512 devices in a mesh: rep: 4 (over y), ep: 128 (over x, z, core).
Axes of the slice: x: 4, y: 4, z: 16, core: 2. Of those that a mesh axis runs over, the one named last changes fastest.
Arguments:
- queries: bfloat16 [16384, 4096], P('ep', 'rep'), may hold values from -8 to 8
- keys: bfloat16 [16384, 512], P('ep', 'rep'), may hold values from -8 to 8
- values: bfloat16 [16384, 512], P('ep', 'rep'), may hold values from -6 to 6
- doc_start: int32 [16384], P('ep'), may hold values from 0 to 16383, as said below
- residual: bfloat16 [128, 128, 2048], P('ep', 'rep'), may hold values from -6 to 6
- out_weight: bfloat16 [4096, 2048], P(('rep', 'ep')), may hold values from -0.09375 to 0.09375
- norm_gain: float32 [2048], replicated, may hold values from 0.1 to 1.9
- gate_weight: bfloat16 [128, 768, 2048], P('ep', 'rep'), may hold values from -0.125 to 0.125
- up_weight: bfloat16 [128, 768, 2048], P('ep', 'rep'), may hold values from -0.125 to 0.125
- down_weight: bfloat16 [128, 768, 2048], P('ep', None, 'rep'), may hold values from -0.21875 to 0.21875
- route_ids: int32 [128, 128, 8], P('ep', 'rep'), may hold values from 0 to 127, all different within a row; in each aligned block of 32 rows (0 to 31, 32 to 63, ..., all dimensions but the last counted through in order) at most 3 rows name the same one
- route_weights: bfloat16 [128, 128, 8], P('ep', 'rep'), may hold values from 0.099609375 to 0.3984375
Outputs:
- updated: bfloat16 [128, 128, 2048], P('ep', 'rep')
The draws below stay inside these ranges and needn't reach their ends.
Inputs may be any that keep to these rules, and one draw needn't show every extreme that they name: `doc_start`: each token's document is a run of consecutive positions of at most 512 tokens that begins at this value; one document has exactly that length. `route_ids`: a token names 8 different experts; in each aligned block of 32 tokens no expert is named more than 3 times, a bound that some block reaches.
All inputs are finite; a program needn't handle non-finite values.
Results may differ from the reference program's by a relative error of at most 0.005.
Values may be sent and summed in bfloat16 or wider, within the bound.
No kernel may reach another device: no remote copies, remote signals or barrier semaphores. Data moves between devices by JAX's collectives and lax.ppermute only.
A program may use at most 64 MiB of HBM per device.

```python
import math
import jax
import jax.numpy as jnp
import numpy as np
from jax import lax

D = 2048
QH = 32
KVH = 4
HS = 128
FF = 768
TOP = 8
HOPS = 4
TOK_EP = 128
SHARDS = 128
TOKENS = 16384
TOK_SUB = 32
EXPERTS = 128
CAP = 3


def document_starts(key):
    base_key = jax.random.fold_in(key, 101)
    longest = HOPS * TOK_EP
    lengths = jax.random.randint(jax.random.fold_in(base_key, 1), (TOKENS,), 1, longest + 1)
    long_index = jax.random.randint(jax.random.fold_in(base_key, 2), (), 0, 2)
    lengths = jnp.where(jnp.arange(TOKENS) == long_index, longest, lengths)
    doc_ends = jnp.cumsum(lengths)
    positions = jnp.arange(TOKENS)
    doc_index = jnp.searchsorted(doc_ends, positions, side='right')
    starts = (doc_ends[doc_index] - lengths[doc_index]).astype(jnp.int32)
    return jnp.where(positions == TOKENS - 1, TOKENS - 1, starts).astype(jnp.int32)


def draw_doc_start(key, part):
    return document_starts(key)


def draw_keys(key, part):
    own_key = jax.random.fold_in(key, 11)
    result_keys = jnp.clip(jax.random.normal(own_key, (TOKENS, KVH * HS), jnp.float32), -6.0, 6.0)
    return result_keys.astype(jnp.bfloat16)


def draw_queries(key, part):
    own_key = jax.random.fold_in(key, 12)
    drawn = jnp.clip(jax.random.normal(own_key, (TOKENS, QH * HS), jnp.float32), -6.0, 6.0)
    return drawn.astype(jnp.bfloat16)


def block_scale(rng, dims, split, least, largest):
    factor_of = 1.0
    for axis_at, blocks in split:
        heights = jax.random.uniform(jax.random.fold_in(jax.random.fold_in(rng, 6), axis_at), (blocks,), jnp.float32, least / len(split), largest / len(split))
        factor_of = factor_of * jnp.repeat(jnp.exp(heights), dims[axis_at] // blocks).reshape((-1,) + (1,) * (len(dims) - 1 - axis_at))
    return factor_of


def deal_out(stream_key, own, number, rows, count, top, reach, lean):
    order = jax.random.permutation(stream_key, count)
    heavy_load, common = load_shares(count, rows * top, reach, lean, True), load_shares(count, rows * top, reach, lean, False)
    places = jnp.arange(count)

    def named(tallies, offset_by):
        used = int((tallies > 0).sum())
        fixed = max(1, used // 4)
        moved = fixed + (places - fixed + offset_by * (used - fixed)) % max(1, count - fixed)
        return jnp.zeros((count,), jnp.int32).at[order[jnp.where(places < fixed, places, moved)]].set(jnp.asarray(tallies, jnp.int32))

    tallies = jnp.where(number % 4 == 0, named(heavy_load, number // 4), named(common, number - number // 4 - 1))
    mixed = jax.random.permutation(jax.random.fold_in(own, 3), count)
    source_of, receiver = mixed[0:count // 2 * 2:2], mixed[1:count // 2 * 2:2]
    room = jnp.minimum(tallies[source_of] - 1, reach - tallies[receiver]) // 2
    room = jnp.where((source_of == order[0]) | (receiver == order[0]) | (tallies[receiver] == 0), 0, jnp.maximum(room, 0))
    moved = jax.random.randint(jax.random.fold_in(own, 4), (count // 2,), 0, 1 << 20) % (room + 1)
    tallies = tallies.at[source_of].add(-moved).at[receiver].add(moved)
    labels = jnp.searchsorted(jnp.cumsum(tallies), jnp.arange(rows * top), side="right").astype(jnp.int32)
    listing = labels.reshape(top, rows).T
    listing = listing[jax.random.permutation(jax.random.fold_in(own, 1), rows)]
    offset_by = jax.random.randint(jax.random.fold_in(own, 2), (rows, 1), 0, top)
    return jnp.take_along_axis(listing, (jnp.arange(top)[None, :] + offset_by) % top, axis=1)


def load_shares(number_of, total, bound, lean, full):
    loads = [(1 << 20) // math.isqrt(grade ** lean) + 1 for grade in range(1, number_of + 1)]
    largest = bound if full else min(bound, max(-(-total // number_of), total * loads[0] // sum(loads)))
    least = 1 if total - largest >= number_of - 1 else 0
    given, spare = [largest] + [least] * (number_of - 1), total - largest - least * (number_of - 1)
    while spare > 0:
        movable = [i for i in range(1, number_of) if given[i] < largest] or [i for i in range(1, number_of) if given[i] < bound]
        mass, left = sum([loads[i] for i in movable]), spare
        for i in movable:
            extra = min(bound - given[i], max(1, left * loads[i] // mass), spare)
            given[i] = given[i] + extra
            spare = spare - extra
    return np.array(given)


def centred(rng, shape, spread, reach, shards=(), held_as=jnp.bfloat16):
    drawn = spread * jax.random.normal(rng, shape, jnp.float32)
    if shards:
        drawn = drawn * block_scale(rng, shape, shards, -0.22, 0.18)
    return jnp.clip(drawn, -reach, reach).astype(held_as)


def setup_inputs(seed: int = 0) -> dict:
    seeds = jax.random.split(jax.random.key(seed), 13)
    queries = draw_queries(jax.random.fold_in(seeds[12], 71), 0)
    keys = draw_keys(jax.random.fold_in(seeds[12], 71), 0)
    values = centred(seeds[2], (TOKENS, KVH * HS), 1.0, 6.0, ((0, 128), (1, 4)))
    doc_start = draw_doc_start(jax.random.fold_in(seeds[12], 71), 0)
    residual = centred(seeds[4], (SHARDS, TOK_EP, D), 1.0, 6.0, ((0, 128), (1, 4)))
    out_weight = centred(seeds[5], (QH * HS, D), (QH * HS) ** -0.5, 0.09375, ((0, 512),))
    norm_gain = jnp.clip(1.0 + 0.18 * jax.random.normal(seeds[6], (D,), jnp.float32), 0.1, 1.9)
    gate_weight = centred(seeds[7], (EXPERTS, FF, D), D ** -0.5, 0.125, ((0, 128), (1, 4)))
    up_weight = centred(seeds[8], (EXPERTS, FF, D), D ** -0.5, 0.125, ((0, 128), (1, 4)))
    down_weight = centred(seeds[9], (EXPERTS, FF, D), FF ** -0.5, 0.21875, ((0, 128), (2, 4)))
    route_ids_keys = jax.random.split(jax.random.fold_in(seeds[10], 1), SHARDS * TOK_EP // TOK_SUB)
    route_ids_turns = jax.random.permutation(jax.random.fold_in(seeds[10], 3), SHARDS * TOK_EP // TOK_SUB)
    route_ids = jax.vmap(lambda own, number: deal_out(jax.random.fold_in(seeds[10], 2), own, number, TOK_SUB, EXPERTS, TOP, CAP, 2))(route_ids_keys, route_ids_turns).reshape((SHARDS, TOK_EP, TOP))
    route_weights = jnp.clip(0.099609375 + 0.29882812 * jax.random.uniform(seeds[11], (SHARDS, TOK_EP, TOP), jnp.float32) ** block_scale(seeds[11], (SHARDS, TOK_EP, TOP), ((0, 128), (1, 4)), -0.2, 0.2), 0.099609375, 0.3984375).astype(jnp.bfloat16)
    return {"queries": queries, "keys": keys, "values": values, "doc_start": doc_start, "residual": residual, "out_weight": out_weight, "norm_gain": norm_gain, "gate_weight": gate_weight, "up_weight": up_weight, "down_weight": down_weight, "route_ids": route_ids, "route_weights": route_weights}


def contract_rows(left, right):
    return lax.dot_general(left, right, (((1,), (1,)), ((), ())), preferred_element_type=jnp.float32)

def reference(queries, keys, values, doc_start, residual, out_weight, norm_gain, gate_weight, up_weight, down_weight, route_ids, route_weights):
    window = HOPS * TOK_EP
    group_size = QH // KVH
    score_scale = 1.0 / HS ** 0.5
    keys_padded = jnp.concatenate([jnp.zeros((window, KVH * HS), keys.dtype), keys], 0)
    values_padded = jnp.concatenate([jnp.zeros((window, KVH * HS), values.dtype), values], 0)

    def one_shard(shard_id):
        begin_row = shard_id * TOK_EP
        query_part = lax.dynamic_slice_in_dim(queries, begin_row, TOK_EP, 0).astype(jnp.float32).reshape(TOK_EP, KVH, group_size, HS)
        key_part = lax.dynamic_slice_in_dim(keys_padded, begin_row, window + TOK_EP, 0).astype(jnp.float32).reshape(-1, KVH, HS)
        value_part = lax.dynamic_slice_in_dim(values_padded, begin_row, window + TOK_EP, 0).astype(jnp.float32).reshape(-1, KVH, HS)
        doc_first = lax.dynamic_slice_in_dim(doc_start, begin_row, TOK_EP, 0)
        query_pos = begin_row + jnp.arange(TOK_EP, dtype=jnp.int32)
        key_pos = begin_row - window + jnp.arange(window + TOK_EP, dtype=jnp.int32)
        key_mask = (key_pos[None, :] <= query_pos[:, None]) & (key_pos[None, :] >= doc_first[:, None])
        score_vals = jnp.einsum('ikgd,jkd->kgij', query_part, key_part) * score_scale
        score_vals = jnp.where(key_mask[None, None], score_vals, -jnp.inf)
        row_peak = lax.optimization_barrier(jnp.max(score_vals, axis=-1, keepdims=True))
        prob_vals = jnp.exp(score_vals - row_peak)
        row_total = lax.optimization_barrier(jnp.sum(prob_vals, axis=-1, keepdims=True))
        prob_low = lax.optimization_barrier(prob_vals.astype(jnp.bfloat16)).astype(jnp.float32)
        weighted = jnp.einsum('kgij,jkd->ikgd', prob_low, value_part)
        weighted = weighted / jnp.transpose(row_total, (2, 0, 1, 3))
        return weighted.reshape(TOK_EP, QH * HS).astype(jnp.bfloat16)
    attended = lax.map(one_shard, jnp.arange(SHARDS, dtype=jnp.int32)).reshape(TOKENS, QH * HS)
    projected = jnp.dot(attended, out_weight, preferred_element_type=jnp.float32)
    hidden_sum = residual.reshape(TOKENS, D).astype(jnp.float32) + projected
    inverse_rms = lax.rsqrt(lax.optimization_barrier(jnp.mean(hidden_sum * hidden_sum, axis=-1, keepdims=True)) + 1e-06)
    normed = (hidden_sum * inverse_rms * norm_gain).astype(jnp.bfloat16)
    expert_ids = route_ids.reshape(TOKENS, TOP)
    gate_vals = route_weights.reshape(TOKENS, TOP).astype(jnp.float32)
    most_rows = TOKENS // TOK_SUB * CAP

    def expert_step(run_total, expert):
        route_hit = expert_ids == expert
        chosen = jnp.any(route_hit, axis=-1)
        row_index = jnp.nonzero(chosen, size=most_rows, fill_value=0)[0].astype(jnp.int32)
        live_count = jnp.sum(chosen.astype(jnp.int32))
        live_rows = (jnp.arange(most_rows, dtype=jnp.int32) < live_count).astype(jnp.float32)
        row_weight = lax.optimization_barrier(jnp.sum(jnp.where(route_hit, gate_vals, 0.0), axis=-1))[row_index] * live_rows
        picked = normed[row_index]
        gate_act = contract_rows(picked, gate_weight[expert])
        up_act = contract_rows(picked, up_weight[expert])
        hidden_act = (jax.nn.silu(gate_act) * up_act).astype(jnp.bfloat16)
        expert_out = jnp.dot(hidden_act, down_weight[expert], preferred_element_type=jnp.float32)
        expert_out = lax.optimization_barrier(expert_out.astype(jnp.bfloat16)).astype(jnp.float32)
        run_total = run_total.at[row_index].add(row_weight[:, None] * expert_out)
        return (run_total, None)
    expert_mix, _ = lax.scan(expert_step, jnp.zeros((TOKENS, D), jnp.float32), jnp.arange(EXPERTS, dtype=jnp.int32))
    return (hidden_sum + expert_mix).astype(jnp.bfloat16).reshape(SHARDS, TOK_EP, D)
```

```python
import jax
import jax.numpy as jnp
from jax import lax
from jax.sharding import Mesh, PartitionSpec as P

HS = 128
HOPS = 4
CAP = 3
BF = jnp.bfloat16
F32 = jnp.float32
EP = ("x", "z", "core")
XC = ("x", "core")


def from_earlier(value, by):
    devices = lax.axis_size(EP)
    return lax.ppermute(value, EP, [(i, i + by) for i in range(devices - by)])


def contract(left, right, dims):
    return lax.dot_general(left, right, (dims, ((), ())), preferred_element_type=F32)


def attention(queries, keys, values, doc_start):
    tok_ep = queries.shape[0]
    group_size = queries.shape[1] // HS
    offset = lax.axis_index(EP) * tok_ep
    own = jnp.concatenate([keys, values], 0)
    blocks = [from_earlier(own, by) for by in range(HOPS, 0, -1)] + [own]
    key_all = jnp.concatenate([b[:tok_ep] for b in blocks], 0)
    value_all = jnp.concatenate([b[tok_ep:] for b in blocks], 0)
    key_pos = offset - HOPS * tok_ep + jnp.arange((HOPS + 1) * tok_ep, dtype=jnp.int32)
    query_pos = offset + jnp.arange(tok_ep, dtype=jnp.int32)
    key_mask = (key_pos[None, :] <= query_pos[:, None]) & (key_pos[None, :] >= doc_start[:, None])
    query_heads = queries.reshape(tok_ep, group_size, HS)
    score_vals = jnp.einsum("igd,jd->gij", query_heads, key_all, preferred_element_type=F32) * (
        1.0 / HS**0.5
    )
    score_vals = jnp.where(key_mask[None], score_vals, -jnp.inf)
    row_peak = jnp.max(score_vals, axis=-1, keepdims=True)
    prob_vals = jnp.exp(score_vals - row_peak)
    row_total = jnp.sum(prob_vals, axis=-1, keepdims=True)
    weighted = jnp.einsum("gij,jd->igd", prob_vals.astype(BF), value_all, preferred_element_type=F32)
    return (
        (weighted / jnp.transpose(row_total, (1, 0, 2))).reshape(tok_ep, group_size * HS).astype(BF)
    )


def on_device(
    queries,
    keys,
    values,
    doc_start,
    residual,
    out_weight,
    norm_gain,
    gate_weight,
    up_weight,
    down_weight,
    route_ids,
    route_weights,
):
    nx, nz, nc, nr = (lax.axis_size(a) for a in ("x", "z", "core", "rep"))
    width = out_weight.shape[1]
    rows8 = out_weight.shape[0]
    tok_sub, top = route_ids.shape[1], route_ids.shape[2]

    out_z = lax.all_gather(out_weight, "z", axis=0, tiled=True)
    out_all = lax.all_gather(out_z, XC, axis=0, tiled=True)

    attended = attention(queries, keys, values, doc_start)
    feats = attended.shape[1]
    place = jnp.arange(feats, dtype=jnp.int32)
    px, pc, pz, pi = (
        place // (nz * nc * rows8),
        (place // (nz * rows8)) % nc,
        (place // rows8) % nz,
        place % rows8,
    )
    source = ((px * nz + pz) * nc + pc) * rows8 + pi
    permute = (place[:, None] == source[None, :]).astype(BF)
    attended = jnp.dot(attended, permute, preferred_element_type=F32).astype(BF)

    gate_weight, up_weight, down_weight, attended = lax.optimization_barrier(
        (gate_weight, up_weight, down_weight, attended)
    )
    gate_all = lax.all_gather(gate_weight[0], "rep", axis=0, tiled=True)
    up_all = lax.all_gather(up_weight[0], "rep", axis=0, tiled=True)
    down_all = lax.all_gather(down_weight[0], "rep", axis=0, tiled=True)

    partial_value = jnp.dot(attended, out_all, preferred_element_type=F32).astype(BF)
    parts = lax.all_to_all(partial_value, "rep", split_axis=0, concat_axis=0, tiled=True)
    head_total = jnp.sum(parts.reshape(nr, tok_sub, width).astype(F32), axis=0)
    hidden_sum = residual[0].astype(F32) + head_total
    inverse_rms = lax.rsqrt(jnp.mean(hidden_sum * hidden_sum, axis=-1, keepdims=True) + 1e-06)
    normed = (hidden_sum * inverse_rms * norm_gain).astype(BF)

    extra = jnp.concatenate([route_ids[0].astype(BF), route_weights[0]], 1)
    extra = jnp.pad(extra, ((0, 0), (0, 128 - 2 * top)))
    column = lax.all_gather(jnp.concatenate([normed, extra], 1), "z", axis=0, tiled=True)
    tokens = column[:, :width]
    info = jnp.transpose(column[:, width : width + 2 * top].astype(F32))
    ids, gains = info[:top].astype(jnp.int32), info[top:]
    count = tokens.shape[0]
    slots = CAP * nz
    local = nx * nc
    lane = jnp.arange(local, dtype=jnp.int32)
    experts = ((lane // nc) * nz + lax.axis_index("z")) * nc + lane % nc
    match = ids[None] == experts[:, None, None]
    hit = jnp.any(match, axis=1)
    gain = jnp.sum(jnp.where(match, gains[None], 0.0), axis=1)
    step = jnp.arange(count, dtype=jnp.int32)
    before = (step[:, None] < step[None, :]).astype(BF)
    rank = jnp.dot(hit.astype(BF), before, preferred_element_type=F32).astype(jnp.int32)
    rank = jnp.where(hit, rank, -1)
    spread = rank[:, None, :] == jnp.arange(slots, dtype=jnp.int32)[None, :, None]
    send_pick = spread.astype(BF).reshape(local * slots, count)
    back_pick = jnp.where(spread, gain[:, None, :], 0.0).astype(BF).reshape(local * slots, count)

    send_rows = jnp.dot(send_pick, tokens, preferred_element_type=F32).astype(BF)
    rows = lax.all_to_all(send_rows, XC, split_axis=0, concat_axis=0, tiled=True)
    gate_act = contract(rows, gate_all, ((1,), (1,)))
    up_act = contract(rows, up_all, ((1,), (1,)))
    hidden_act = (jax.nn.silu(gate_act) * up_act).astype(BF)
    down_parts = down_all.reshape(nr, -1, down_all.shape[1])
    expert_out = jnp.concatenate(
        [
            jnp.dot(hidden_act, down_parts[r], preferred_element_type=F32).astype(BF)
            for r in range(nr)
        ],
        1,
    )
    returned = lax.all_to_all(expert_out, XC, split_axis=0, concat_axis=0, tiled=True)
    mixed = contract(back_pick, returned, ((0,), (0,))).astype(BF)
    expert_mix = lax.psum_scatter(mixed, "z", scatter_dimension=0, tiled=True)
    return (hidden_sum + expert_mix.astype(F32)).astype(BF)[None]


def solution(mesh):
    devices = mesh.devices
    split = Mesh(devices.reshape(4, 4, devices.shape[1] // 8, 2), ("rep",) + EP)
    placed = (
        P(EP, "rep"),
        P(EP, "rep"),
        P(EP, "rep"),
        P(EP),
        P(EP, "rep", None),
        P(("rep",) + EP, None),
        P(),
        P(EP, "rep", None),
        P(EP, "rep", None),
        P(EP, None, "rep"),
        P(EP, "rep", None),
        P(EP, "rep", None),
    )
    return jax.shard_map(
        on_device, mesh=split, in_specs=placed, out_specs=P(EP, "rep", None), check_vma=False
    )
```

```python
import jax
import jax.numpy as jnp
from jax import lax
from jax.sharding import Mesh, PartitionSpec as P

HS = 128
HOPS = 4
CAP = 3
BF = jnp.bfloat16
F32 = jnp.float32
EP = ("x", "z", "core")
XC = ("x", "core")


def from_earlier(value, by):
    devices = lax.axis_size(EP)
    return lax.ppermute(value, EP, [(i, i + by) for i in range(devices - by)])


def shift(value, axis, by):
    devices = lax.axis_size(axis)
    return lax.ppermute(value, axis, [(i, (i + by) % devices) for i in range(devices)])


def other_core(value):
    return shift(value, "core", 1)


def contract(left, right, dims):
    return lax.dot_general(left, right, (dims, ((), ())), preferred_element_type=F32)


def gather_x(value):
    half = value.shape[0] // 2
    from_left, from_right = shift(value, "x", 1), shift(value, "x", -1)
    far_low, far_high = shift(from_left[:half], "x", 1), shift(from_right[half:], "x", -1)
    return jnp.concatenate([value, from_left, from_right, far_low, far_high], 0)


def ring_blocks(value, axis):
    devices = lax.axis_size(axis)
    blocks = {0: value}
    right = left = value
    for step in range(1, devices // 2 + 1):
        right = shift(right, axis, 1)
        blocks[devices - step] = right
        if step < devices - step:
            left = shift(left, axis, -1)
            blocks[step] = left
    return blocks


def attention(queries, keys, values, doc_start):
    tok_ep = queries.shape[0]
    group_size = queries.shape[1] // HS
    offset = lax.axis_index(EP) * tok_ep
    own = jnp.concatenate([keys, values], 0)
    blocks = [from_earlier(own, by) for by in range(HOPS, 0, -1)] + [own]
    key_all = jnp.concatenate([b[:tok_ep] for b in blocks], 0)
    value_all = jnp.concatenate([b[tok_ep:] for b in blocks], 0)
    key_pos = offset - HOPS * tok_ep + jnp.arange((HOPS + 1) * tok_ep, dtype=jnp.int32)
    query_pos = offset + jnp.arange(tok_ep, dtype=jnp.int32)
    key_mask = (key_pos[None, :] <= query_pos[:, None]) & (key_pos[None, :] >= doc_start[:, None])
    query_heads = queries.reshape(tok_ep, group_size, HS)
    score_vals = jnp.einsum("igd,jd->gij", query_heads, key_all, preferred_element_type=F32) * (
        1.0 / HS**0.5
    )
    score_vals = jnp.where(key_mask[None], score_vals, -jnp.inf)
    row_peak = jnp.max(score_vals, axis=-1, keepdims=True)
    prob_vals = jnp.exp(score_vals - row_peak)
    row_total = jnp.sum(prob_vals, axis=-1, keepdims=True)
    weighted = jnp.einsum("gij,jd->igd", prob_vals.astype(BF), value_all, preferred_element_type=F32)
    return (
        (weighted / jnp.transpose(row_total, (1, 0, 2))).reshape(tok_ep, group_size * HS).astype(BF)
    )


def picks(ids, gains, experts, slots):
    count = ids.shape[1]
    match = ids[None] == experts[:, None, None]
    hit = jnp.any(match, axis=1)
    gain = jnp.sum(jnp.where(match, gains[None], 0.0), axis=1)
    step = jnp.arange(count, dtype=jnp.int32)
    before = (step[:, None] < step[None, :]).astype(BF)
    rank = jnp.dot(hit.astype(BF), before, preferred_element_type=F32).astype(jnp.int32)
    rank = jnp.where(hit, rank, -1)
    spread = rank[:, None, :] == jnp.arange(slots, dtype=jnp.int32)[None, :, None]
    send = spread.astype(BF).reshape(-1, count)
    back = jnp.where(spread, gain[:, None, :], 0.0).astype(BF).reshape(-1, count)
    return send, back


def on_device(
    queries,
    keys,
    values,
    doc_start,
    residual,
    out_weight,
    norm_gain,
    gate_weight,
    up_weight,
    down_weight,
    route_ids,
    route_weights,
):
    nx, nz, nc, nr = (lax.axis_size(a) for a in ("x", "z", "core", "rep"))
    width = out_weight.shape[1]
    rows8 = out_weight.shape[0]
    tok_sub, top = route_ids.shape[1], route_ids.shape[2]
    here = lax.axis_index("z")

    gate_all = lax.all_gather(gate_weight[0], "rep", axis=0, tiled=True)
    up_all = lax.all_gather(up_weight[0], "rep", axis=0, tiled=True)
    down_all = lax.all_gather(down_weight[0], "rep", axis=0, tiled=True)

    info = jnp.concatenate([route_ids[0].astype(BF), route_weights[0]], 1)
    info = jnp.transpose(info).reshape(rows8, -1)
    info_width = info.shape[1]
    info = jnp.pad(info, ((0, 0), (0, -info_width % 128)))
    z_all = lax.all_gather(jnp.concatenate([out_weight, info], 1), "z", axis=0, tiled=True)
    z_rows = z_all[:, :width]
    z_rows, keys, values = lax.optimization_barrier((z_rows, keys, values))
    out_own = gather_x(z_rows)
    out_other = other_core(out_own)

    attended = attention(queries, keys, values, doc_start)
    feats = attended.shape[1]
    place = jnp.arange(feats, dtype=jnp.int32)
    block = nz * rows8
    hop = (place // block) % nx
    pc = place // (block * nx)
    pc = jnp.where(lax.axis_index("core") == 0, pc, nc - 1 - pc)
    px = (lax.axis_index("x") + nx + jnp.where(hop == 1, -1, jnp.where(hop == 2, 1, hop // 3 * 2))) % nx
    pz, pi = (place // rows8) % nz, place % rows8
    source = ((px * nz + pz) * nc + pc) * rows8 + pi
    permute = (place[:, None] == source[None, :]).astype(BF)
    attended = jnp.dot(attended, permute, preferred_element_type=F32).astype(BF)

    half = feats // 2
    partial_value = jnp.dot(attended[:, :half], out_own, preferred_element_type=F32)
    partial_value += jnp.dot(attended[:, half:], out_other, preferred_element_type=F32)
    partial_value = partial_value.astype(BF)
    parts = lax.all_to_all(partial_value, "rep", split_axis=0, concat_axis=0, tiled=True)
    head_total = jnp.sum(parts.reshape(nr, tok_sub, width).astype(F32), axis=0)
    hidden_sum = residual[0].astype(F32) + head_total
    inverse_rms = lax.rsqrt(jnp.mean(hidden_sum * hidden_sum, axis=-1, keepdims=True) + 1e-06)
    normed = (hidden_sum * inverse_rms * norm_gain).astype(BF)

    table = z_all[:, width : width + info_width].reshape(nz, 2 * top, tok_sub)
    table = lax.dynamic_slice_in_dim(jnp.concatenate([table, table], 0), here, nz, 0)
    table = jnp.transpose(table.astype(F32), (1, 0, 2))
    lane = jnp.arange(nx * nc, dtype=jnp.int32)
    experts = ((lane // nc) * nz + here) * nc + lane % nc
    near, quarter = [], nz // 4
    near = list(range(quarter)) + list(range(nz - quarter, nz))
    far = list(range(quarter, nz - quarter))
    groups = []
    for members in (near, far):
        part = jnp.concatenate([table[:, m] for m in members], 1)
        send, back = picks(part[:top].astype(jnp.int32), part[top:], experts, CAP * len(members))
        block_at = (here + jnp.array(members, jnp.int32)) % nz
        token_at = (block_at[:, None] * tok_sub + jnp.arange(tok_sub, dtype=jnp.int32)).reshape(-1)
        all_at = jnp.arange(nz * tok_sub, dtype=jnp.int32)
        reorder = (token_at[:, None] == all_at[None, :]).astype(BF)
        back = jnp.dot(back, reorder, preferred_element_type=F32).astype(BF)
        groups.append((members, send, back))

    blocks = ring_blocks(normed, "z")
    down_parts = down_all.reshape(nr, -1, down_all.shape[1])
    backs, returned = [], []
    for members, send, back in groups:
        tokens = jnp.concatenate([blocks[m] for m in members], 0)
        send_rows = jnp.dot(send, tokens, preferred_element_type=F32).astype(BF)
        rows = lax.all_to_all(send_rows, XC, split_axis=0, concat_axis=0, tiled=True)
        gate_act = contract(rows, gate_all, ((1,), (1,)))
        up_act = contract(rows, up_all, ((1,), (1,)))
        hidden_act = (jax.nn.silu(gate_act) * up_act).astype(BF)
        expert_out = jnp.concatenate(
            [
                jnp.dot(hidden_act, down_parts[r], preferred_element_type=F32).astype(BF)
                for r in range(nr)
            ],
            1,
        )
        returned.append(lax.all_to_all(expert_out, XC, split_axis=0, concat_axis=0, tiled=True))
        backs.append(back)
    mixed = contract(jnp.concatenate(backs, 0), jnp.concatenate(returned, 0), ((0,), (0,))).astype(BF)
    expert_mix = lax.psum_scatter(mixed, "z", scatter_dimension=0, tiled=True)
    return (hidden_sum + expert_mix.astype(F32)).astype(BF)[None]


def solution(mesh):
    devices = mesh.devices
    split = Mesh(devices.reshape(4, 4, devices.shape[1] // 8, 2), ("rep",) + EP)
    placed = (
        P(EP, "rep"),
        P(EP, "rep"),
        P(EP, "rep"),
        P(EP),
        P(EP, "rep", None),
        P(("rep",) + EP, None),
        P(),
        P(EP, "rep", None),
        P(EP, "rep", None),
        P(EP, None, "rep"),
        P(EP, "rep", None),
        P(EP, "rep", None),
    )
    return jax.shard_map(
        on_device, mesh=split, in_specs=placed, out_specs=P(EP, "rep", None), check_vma=False
    )
```

```python
import functools

import jax
import jax.numpy as jnp
from jax import lax
from jax.experimental import pallas as pl
from jax.experimental.pallas import tpu as pltpu
from jax.sharding import Mesh, PartitionSpec as P

HS = 128
HOPS = 4
CAP = 3
BF = jnp.bfloat16
F16 = jnp.float16
F32 = jnp.float32
EP = ("x", "z", "core")
XC = ("x", "core")
XZ = ("x", "z")
ZC = ("z", "core")


def from_earlier(value, by):
    chips = lax.axis_size(XZ)
    return lax.ppermute(value, XZ, [(i, i + by) for i in range(chips - by)])


def shift(value, axis, by):
    devices = lax.axis_size(axis)
    return lax.ppermute(value, axis, [(i, (i + by) % devices) for i in range(devices)])


def other_core(value):
    return shift(value, "core", 1)


def contract(left, right, dims):
    return lax.dot_general(left, right, (dims, ((), ())), preferred_element_type=F32)


def gather_x(value):
    half = value.shape[0] // 2
    from_left, from_right = shift(value, "x", 1), shift(value, "x", -1)
    far_low, far_high = shift(from_left[:half], "x", 1), shift(from_right[half:], "x", -1)
    return jnp.concatenate([value, from_left, from_right, far_low, far_high], 0)


def attention(queries, keys, values, doc_start):
    tok_ep = queries.shape[0]
    group_size = queries.shape[1] // HS
    cores = lax.axis_size("core")
    chips = -(-HOPS // cores)
    own = lax.all_gather(jnp.concatenate([keys, values], 1), "core", axis=0, tiled=True)
    both = jnp.concatenate([from_earlier(own, by) for by in range(chips, 0, -1)] + [own], 0)
    key_all, value_all = both[:, :HS], both[:, HS:]
    first = (lax.axis_index(XZ) - chips) * cores * tok_ep
    key_pos = first + jnp.arange(both.shape[0], dtype=jnp.int32)
    query_pos = lax.axis_index(EP) * tok_ep + jnp.arange(tok_ep, dtype=jnp.int32)
    key_mask = (key_pos[None, :] <= query_pos[:, None]) & (key_pos[None, :] >= doc_start[:, None])
    query_heads = queries.reshape(tok_ep, group_size, HS)
    score_vals = jnp.einsum("igd,jd->gij", query_heads, key_all, preferred_element_type=F32) * (
        1.0 / HS**0.5
    )
    score_vals = jnp.where(key_mask[None], score_vals, -jnp.inf)
    row_peak = jnp.max(score_vals, axis=-1, keepdims=True)
    prob_vals = jnp.exp(score_vals - row_peak)
    row_total = jnp.sum(prob_vals, axis=-1, keepdims=True)
    weighted = jnp.einsum("gij,jd->igd", prob_vals.astype(BF), value_all, preferred_element_type=F32)
    return (
        (weighted / jnp.transpose(row_total, (1, 0, 2))).reshape(tok_ep, group_size * HS).astype(BF)
    )


def slot_ranks(ids, experts, core_of):
    match = ids[None] == experts[:, None, None]
    hit = jnp.any(match, axis=1)
    step = jnp.arange(ids.shape[1], dtype=jnp.int32)
    before = (step[:, None] < step[None, :]) & (core_of[:, None] == core_of[None, :])
    rank = jnp.dot(hit.astype(BF), before.astype(BF), preferred_element_type=F32).astype(jnp.int32)
    return match, jnp.where(hit, rank, -1)


def expert_kernel(parts, rows_ref, gate_up_ref, down_ref, out_ref, hidden_ref):
    step = pl.program_id(0)
    units = gate_up_ref.shape[0] // 2

    @pl.when(step < parts)
    def _():
        rows = rows_ref[...]
        gate = contract(rows, gate_up_ref[:units], ((1,), (1,)))
        up = contract(rows, gate_up_ref[units:], ((1,), (1,)))
        hidden_ref[step] = (gate / (1.0 + jnp.exp(-gate)) * up).astype(BF)

    @pl.when(step >= parts)
    def _():
        total = jnp.dot(hidden_ref[0], down_ref[:units], preferred_element_type=F32)
        for part in range(1, parts):
            rows_of = pl.ds(part * units, units)
            total += jnp.dot(hidden_ref[part], down_ref[rows_of], preferred_element_type=F32)
        out_ref[...] = total.astype(BF)


def expert(rows, gate_up, down, parts):
    count, width = rows.shape
    units, cols = gate_up.shape[0] // parts, down.shape[1]
    return pl.pallas_call(
        functools.partial(expert_kernel, parts),
        grid=(2 * parts,),
        in_specs=[
            pl.BlockSpec((count, width), lambda i: (0, 0)),
            pl.BlockSpec((units, width), lambda i: (jnp.minimum(i, parts - 1), 0)),
            pl.BlockSpec((down.shape[0] // parts, cols), lambda i: (jnp.maximum(i - parts, 0), 0)),
        ],
        out_specs=pl.BlockSpec((count, cols), lambda i: (0, jnp.maximum(i - parts, 0))),
        out_shape=jax.ShapeDtypeStruct((count, width), BF),
        scratch_shapes=[pltpu.VMEM((parts, count, units // 2), BF)],
        compiler_params=pltpu.CompilerParams(vmem_limit_bytes=40 * 2**20),
        cost_estimate=pl.CostEstimate(
            flops=2 * count * (gate_up.size + down.size),
            bytes_accessed=2 * (2 * rows.size + gate_up.size + down.size),
            transcendentals=count * gate_up.shape[0] // 2,
        ),
    )(rows, gate_up, down)


def on_device(
    queries,
    keys,
    values,
    doc_start,
    residual,
    out_weight,
    norm_gain,
    gate_weight,
    up_weight,
    down_weight,
    route_ids,
    route_weights,
):
    nx, nz, nc, nr = (lax.axis_size(a) for a in ("x", "z", "core", "rep"))
    width = out_weight.shape[1]
    rows8 = out_weight.shape[0]
    tok_sub, top = route_ids.shape[1], route_ids.shape[2]
    here = lax.axis_index("z")

    gate_up = jnp.concatenate([gate_weight[0], up_weight[0]], 0)
    gate_up = lax.all_gather(gate_up, "rep", axis=0, tiled=True)

    info = jnp.concatenate([route_ids[0].astype(F16), route_weights[0].astype(F16)], 1)
    info = info.reshape(rows8, -1)
    info_width = info.shape[1]
    info = jnp.pad(info, ((0, 0), (0, -info_width % 128)))
    z_all = lax.all_gather(
        jnp.concatenate([out_weight.astype(F16), info], 1), ZC, axis=0, tiled=True
    )
    z_rows = z_all[:, :width].reshape(nz, nc, rows8, width)
    z_rows = lax.dynamic_slice_in_dim(z_rows, lax.axis_index("core"), 1, 1)
    z_rows = z_rows.reshape(nz * rows8, width).astype(BF)
    z_rows, keys, values = lax.optimization_barrier((z_rows, keys, values))
    out_own = gather_x(z_rows)
    out_other = other_core(out_own)

    attended = attention(queries, keys, values, doc_start)
    feats = attended.shape[1]
    place = jnp.arange(feats, dtype=jnp.int32)
    block = nz * rows8
    hop = (place // block) % nx
    pc = place // (block * nx)
    pc = jnp.where(lax.axis_index("core") == 0, pc, nc - 1 - pc)
    px = (lax.axis_index("x") + nx + jnp.where(hop == 1, -1, jnp.where(hop == 2, 1, hop // 3 * 2))) % nx
    pz, pi = (place // rows8) % nz, place % rows8
    source = ((px * nz + pz) * nc + pc) * rows8 + pi
    permute = (place[:, None] == source[None, :]).astype(BF)
    attended = jnp.dot(attended, permute, preferred_element_type=F32).astype(BF)

    half = feats // 2
    partial_value = jnp.dot(attended[:, :half], out_own, preferred_element_type=F32)
    partial_value += jnp.dot(attended[:, half:], out_other, preferred_element_type=F32)
    partial_value = partial_value.astype(BF)
    parts = lax.all_to_all(partial_value, "rep", split_axis=0, concat_axis=0, tiled=True)
    parts, gate_up, down_weight = lax.optimization_barrier((parts, gate_up, down_weight))
    down_all = lax.all_gather(down_weight[0], "rep", axis=0, tiled=True)
    head_total = jnp.sum(parts.reshape(nr, tok_sub, width).astype(F32), axis=0)
    hidden_sum = residual[0].astype(F32) + head_total
    inverse_rms = lax.rsqrt(jnp.mean(hidden_sum * hidden_sum, axis=-1, keepdims=True) + 1e-06)
    normed = (hidden_sum * inverse_rms * norm_gain).astype(BF)
    column = lax.all_gather(normed.astype(F16), ZC, axis=0, tiled=True).astype(BF)

    table = z_all[:, width : width + info_width].astype(F32).reshape(-1, 2 * top)
    table = jnp.transpose(table)
    count = table.shape[1]
    core = lax.axis_index("core")
    core_of = jnp.arange(count, dtype=jnp.int32) // tok_sub % nc
    slot = jnp.arange(CAP * nz, dtype=jnp.int32)
    ids = table[:top].astype(jnp.int32)
    experts = (jnp.arange(nx, dtype=jnp.int32) * nz + here) * nc + core
    _, rank = slot_ranks(ids, experts, core_of)
    seat = core_of[None, :] * slot.size + rank
    seat = jnp.where(rank < 0, -1, seat)
    seats = jnp.arange(nc * slot.size, dtype=jnp.int32)
    send = (seat[:, None, :] == seats[None, :, None]).astype(BF).reshape(-1, count)

    table = table.reshape(2 * top, nz, nc, tok_sub)
    table = lax.dynamic_slice_in_dim(table, core, 1, 2).reshape(2 * top, -1)
    lane = jnp.arange(nx * nc, dtype=jnp.int32)
    experts = ((lane // nc) * nz + here) * nc + lane % nc
    own_count = table.shape[1]
    match, rank = slot_ranks(
        table[:top].astype(jnp.int32), experts, jnp.zeros((own_count,), jnp.int32)
    )
    gain = jnp.sum(jnp.where(match, table[None, top:], 0.0), axis=1)
    back = jnp.where(rank[:, None, :] == slot[None, :, None], gain[:, None, :], 0.0)
    back = back.astype(BF).reshape(-1, own_count)

    send_rows = jnp.dot(send, column, preferred_element_type=F32).astype(BF)
    rows = lax.all_to_all(send_rows, "x", split_axis=0, concat_axis=0, tiled=True)
    expert_out = expert(rows, gate_up, down_all, nr)
    returned = lax.all_to_all(expert_out, XC, split_axis=0, concat_axis=0, tiled=True)
    mixed = contract(back, returned, ((0,), (0,))).astype(BF)
    expert_mix = lax.psum_scatter(mixed, "z", scatter_dimension=0, tiled=True)
    return (hidden_sum + expert_mix.astype(F32)).astype(BF)[None]


def solution(mesh):
    devices = mesh.devices
    split = Mesh(devices.reshape(4, 4, devices.shape[1] // 8, 2), ("rep",) + EP)
    placed = (
        P(EP, "rep"),
        P(EP, "rep"),
        P(EP, "rep"),
        P(EP),
        P(EP, "rep", None),
        P(("rep",) + EP, None),
        P(),
        P(EP, "rep", None),
        P(EP, "rep", None),
        P(EP, None, "rep"),
        P(EP, "rep", None),
        P(EP, "rep", None),
    )
    return jax.shard_map(
        on_device, mesh=split, in_specs=placed, out_specs=P(EP, "rep", None), check_vma=False
    )
```

```python
import functools

import jax
import jax.numpy as jnp
from jax import lax
from jax.experimental import pallas as pl
from jax.experimental.pallas import tpu as pltpu
from jax.sharding import Mesh, PartitionSpec as P

HS = 128
HOPS = 4
CAP = 3
VMEM_GRANT = 56 * 2**20
BF = jnp.bfloat16
F16 = jnp.float16
F32 = jnp.float32
X = ("xh", "xl")
EP = ("xh", "xl", "z", "core")
XC = ("xh", "xl", "core")
XZ = ("xh", "xl", "z")
ZC = ("z", "core")


def from_earlier(value, by):
    chips = lax.axis_size(XZ)
    return lax.ppermute(value, XZ, [(i, i + by) for i in range(chips - by)])


def shift(value, axis, by):
    devices = lax.axis_size(axis)
    return lax.ppermute(value, axis, [(i, (i + by) % devices) for i in range(devices)])


def contract(left, right, dims):
    return lax.dot_general(left, right, (dims, ((), ())), preferred_element_type=F32)


def attention(queries, keys, values, doc_start):
    tok_ep = queries.shape[0]
    group_size = queries.shape[1] // HS
    cores = lax.axis_size("core")
    chips = -(-HOPS // cores)
    own = lax.all_gather(jnp.concatenate([keys, values], 1), "core", axis=0, tiled=True)
    both = jnp.concatenate([from_earlier(own, by) for by in range(chips, 0, -1)] + [own], 0)
    key_all, value_all = both[:, :HS], both[:, HS:]
    first = (lax.axis_index(XZ) - chips) * cores * tok_ep
    key_pos = first + jnp.arange(both.shape[0], dtype=jnp.int32)
    query_pos = lax.axis_index(EP) * tok_ep + jnp.arange(tok_ep, dtype=jnp.int32)
    key_mask = (key_pos[None, :] <= query_pos[:, None]) & (key_pos[None, :] >= doc_start[:, None])
    query_heads = queries.reshape(tok_ep, group_size, HS)
    score_vals = jnp.einsum("igd,jd->gij", query_heads, key_all, preferred_element_type=F32) * (
        1.0 / HS**0.5
    )
    score_vals = jnp.where(key_mask[None], score_vals, -jnp.inf)
    row_peak = jnp.max(score_vals, axis=-1, keepdims=True)
    prob_vals = jnp.exp(score_vals - row_peak)
    row_total = jnp.sum(prob_vals, axis=-1, keepdims=True)
    weighted = jnp.einsum("gij,jd->igd", prob_vals.astype(BF), value_all, preferred_element_type=F32)
    return (
        (weighted / jnp.transpose(row_total, (1, 0, 2))).reshape(tok_ep, group_size * HS).astype(BF)
    )


def slot_ranks(ids, experts, core_of):
    match = ids[None] == experts[:, None, None]
    hit = jnp.any(match, axis=1)
    step = jnp.arange(ids.shape[1], dtype=jnp.int32)
    before = (step[:, None] < step[None, :]) & (core_of[:, None] == core_of[None, :])
    rank = jnp.dot(hit.astype(BF), before.astype(BF), preferred_element_type=F32).astype(jnp.int32)
    return match, jnp.where(hit, rank, -1)


def expert_kernel(parts, rows_ref, gate_up_ref, down_ref, out_ref, gu_ref, dn_ref, hidden_ref, sems):
    units, cols = gu_ref.shape[1] // 2, dn_ref.shape[2]
    copies = [
        pltpu.make_async_copy(gate_up_ref.at[part], gu_ref.at[part], sems.at[part])
        for part in range(parts)
    ] + [
        pltpu.make_async_copy(down_ref.at[part], dn_ref.at[part], sems.at[parts + part])
        for part in range(parts)
    ]
    for copy in copies:
        copy.start()
    rows = rows_ref[...]
    for part in range(0, parts, 2):
        copies[part].wait()
        copies[part + 1].wait()
        both = gu_ref[part : part + 2].reshape(4 * units, rows.shape[1])
        act = contract(rows, both, ((1,), (1,)))
        for k in range(2):
            gate = act[:, 2 * k * units : (2 * k + 1) * units]
            up = act[:, (2 * k + 1) * units : (2 * k + 2) * units]
            hidden = (gate / (1.0 + jnp.exp(-gate)) * up).astype(BF)
            hidden_ref[:, (part + k) * units : (part + k + 1) * units] = hidden
    hidden = hidden_ref[...]
    for part in range(parts):
        copies[parts + part].wait()
        total = jnp.dot(hidden, dn_ref[part], preferred_element_type=F32)
        out_ref[:, part * cols : (part + 1) * cols] = total.astype(BF)


def expert(rows, gate_up, down, parts):
    count, width = rows.shape
    gate_up = gate_up.reshape(parts, -1, width)
    down = down.reshape(parts, -1, down.shape[1])
    return pl.pallas_call(
        functools.partial(expert_kernel, parts),
        in_specs=[
            pl.BlockSpec(memory_space=pltpu.VMEM),
            pl.BlockSpec(memory_space=pltpu.HBM),
            pl.BlockSpec(memory_space=pltpu.HBM),
        ],
        out_specs=pl.BlockSpec(memory_space=pltpu.VMEM),
        out_shape=jax.ShapeDtypeStruct((count, width), BF),
        scratch_shapes=[
            pltpu.VMEM(gate_up.shape, BF),
            pltpu.VMEM(down.shape, BF),
            pltpu.VMEM((count, parts * gate_up.shape[1] // 2), BF),
            pltpu.SemaphoreType.DMA((2 * parts,)),
        ],
        compiler_params=pltpu.CompilerParams(vmem_limit_bytes=VMEM_GRANT),
        cost_estimate=pl.CostEstimate(
            flops=2 * count * (gate_up.size + down.size),
            bytes_accessed=2 * (2 * rows.size + gate_up.size + down.size),
            transcendentals=count * gate_up.shape[1] * parts // 2,
        ),
    )(rows, gate_up, down)


def add_low(left, right):
    return (left.astype(F32) + right.astype(F32)).astype(BF)


def ring_sums(chunks):
    places = len(chunks)

    def two(k):
        return jnp.concatenate([chunks[k % places], chunks[(k - 1) % places]], 0)

    def two_back(k):
        return jnp.concatenate([chunks[-k % places], chunks[(1 - k) % places]], 0)

    rows = chunks[0].shape[0]
    half = places // 2
    right, left = two(half), two_back(half - 1)
    for k in range(half - 2, 0, -2):
        right = add_low(shift(right, "z", 2), two(k))
        left = shift(left, "z", -2)
        if k > 2:
            left = add_low(left, two_back(k - 1))
    last = shift(add_low(left[:rows], chunks[-1]), "z", -1)
    pieces = [left[rows:], shift(right[:rows], "z", 2), shift(right[rows:], "z", 1), last]
    return sum((p.astype(F32) for p in pieces), chunks[0].astype(F32))


def on_device(
    queries,
    keys,
    values,
    doc_start,
    residual,
    out_weight,
    norm_gain,
    gate_weight,
    up_weight,
    down_weight,
    route_ids,
    route_weights,
):
    nx, nz, nc, nr = (lax.axis_size(a) for a in (X, "z", "core", "rep"))
    width = out_weight.shape[1]
    rows8 = out_weight.shape[0]
    tok_sub, top = route_ids.shape[1], route_ids.shape[2]
    here = lax.axis_index("z")

    gate_up = jnp.concatenate([gate_weight[0], up_weight[0]], 0)
    gate_up = lax.all_gather(gate_up, "rep", axis=0, tiled=True)

    info = jnp.concatenate([route_ids[0].astype(F16), route_weights[0].astype(F16)], 1)
    info = jnp.pad(info, ((0, 0), (0, 128 - 2 * top)))
    groups = tok_sub // rows8
    own_rows = jnp.concatenate(
        [out_weight.astype(F16)] + [info[g * rows8 : (g + 1) * rows8] for g in range(groups)], 1
    )
    pair_rows = jnp.concatenate([own_rows, shift(own_rows, "xl", 1)], 0)

    attended = attention(queries, keys, values, doc_start)
    half = attended.shape[1] // 2
    xh = lax.axis_index("xh")
    low, high = attended[:, :half], attended[:, half:]
    kept = jnp.where(xh == 0, low, high)
    given = jnp.where(xh == 0, high, low)
    got = shift(given, "xh", 1)
    pair_rows, _ = lax.optimization_barrier((pair_rows, given))
    z_all = lax.all_gather(pair_rows, ZC, axis=0, tiled=True)
    out_rows = z_all[:, :width].astype(BF)

    both = jnp.stack([jnp.where(xh == 0, kept, got), jnp.where(xh == 0, got, kept)], 0)
    both = both.reshape(2, nr, tok_sub, half).transpose(1, 0, 2, 3).reshape(-1, half)
    place = jnp.arange(half, dtype=jnp.int32)
    pi, px = place % rows8, place // rows8 % 2
    px = jnp.where(lax.axis_index("xl") == 0, px, 1 - px)
    pc, pz = place // (2 * rows8) % nc, place // (2 * rows8 * nc)
    source = ((px * nz + pz) * nc + pc) * rows8 + pi
    permute = (place[:, None] == source[None, :]).astype(BF)
    both = jnp.dot(both, permute, preferred_element_type=F32).astype(BF)
    partial_value = jnp.dot(both, out_rows, preferred_element_type=F32).astype(BF)
    parts = lax.all_to_all(partial_value, ("rep", "xh"), split_axis=0, concat_axis=0, tiled=True)
    parts, gate_up, down_weight = lax.optimization_barrier((parts, gate_up, down_weight))
    down_all = lax.all_gather(down_weight[0], "rep", axis=0, tiled=True)
    head_total = jnp.sum(parts.reshape(-1, tok_sub, width).astype(F32), axis=0)
    hidden_sum = residual[0].astype(F32) + head_total
    inverse_rms = lax.rsqrt(jnp.mean(hidden_sum * hidden_sum, axis=-1, keepdims=True) + 1e-06)
    normed = (hidden_sum * inverse_rms * norm_gain).astype(BF)
    column = lax.all_gather(normed.astype(F16), ZC, axis=0, tiled=True).astype(BF)

    table = z_all.reshape(nz * nc, 2, rows8, -1)[:, 0].reshape(nz * nc * rows8, -1)
    table = [table[:, width + 128 * g :][:, : 2 * top].astype(F32) for g in range(groups)]
    table = jnp.stack([jnp.transpose(t).reshape(2 * top, -1, rows8) for t in table], 2)
    table = table.reshape(2 * top, -1)
    count = table.shape[1]
    core = lax.axis_index("core")
    core_of = jnp.arange(count, dtype=jnp.int32) // tok_sub % nc
    slot = jnp.arange(CAP * nz, dtype=jnp.int32)
    ids = table[:top].astype(jnp.int32)
    experts = (jnp.arange(nx, dtype=jnp.int32) * nz + here) * nc + core
    _, rank = slot_ranks(ids, experts, core_of)
    seat = core_of[None, :] * slot.size + rank
    seat = jnp.where(rank < 0, -1, seat)
    seats = jnp.arange(nc * slot.size, dtype=jnp.int32)
    send = (seat[:, None, :] == seats[None, :, None]).astype(BF).reshape(-1, count)

    table = table.reshape(2 * top, nz, nc, tok_sub)
    table = lax.dynamic_slice_in_dim(table, core, 1, 2).reshape(2 * top, -1)
    lane = jnp.arange(nx * nc, dtype=jnp.int32)
    experts = ((lane // nc) * nz + here) * nc + lane % nc
    own_count = table.shape[1]
    match, rank = slot_ranks(
        table[:top].astype(jnp.int32), experts, jnp.zeros((own_count,), jnp.int32)
    )
    gain = jnp.sum(jnp.where(match, table[None, top:], 0.0), axis=1)

    def back_for(rank, gain):
        back = jnp.where(rank[:, None, :] == slot[None, :, None], gain[:, None, :], 0.0)
        return back.astype(BF).reshape(-1, own_count)

    def from_here(value):
        value = value.reshape(-1, nz, tok_sub)
        value = lax.dynamic_slice_in_dim(jnp.concatenate([value, value], 1), here, nz, 1)
        return value.reshape(-1, own_count)

    back = back_for(from_here(rank), from_here(gain))

    send_rows = jnp.dot(send, column, preferred_element_type=F32).astype(BF)
    rows = lax.all_to_all(send_rows, X, split_axis=0, concat_axis=0, tiled=True)
    expert_out = expert(rows, gate_up, down_all, nr)
    returned = lax.all_to_all(expert_out, XC, split_axis=0, concat_axis=0, tiled=True)
    mixed = contract(back, returned, ((0,), (0,))).astype(BF)
    expert_mix = ring_sums([mixed[k * tok_sub : (k + 1) * tok_sub] for k in range(nz)])
    return (hidden_sum + expert_mix).astype(BF)[None]


def solution(mesh):
    devices = mesh.devices
    split = Mesh(devices.reshape(4, 2, 2, devices.shape[1] // 8, 2), ("rep",) + EP)
    placed = (
        P(EP, "rep"),
        P(EP, "rep"),
        P(EP, "rep"),
        P(EP),
        P(EP, "rep", None),
        P(("rep",) + EP, None),
        P(),
        P(EP, "rep", None),
        P(EP, "rep", None),
        P(EP, None, "rep"),
        P(EP, "rep", None),
        P(EP, "rep", None),
    )
    return jax.shard_map(
        on_device, mesh=split, in_specs=placed, out_specs=P(EP, "rep", None), check_vma=False
    )
```

```python
import functools

import jax
import jax.numpy as jnp
from jax import lax
from jax.experimental import pallas as pl
from jax.experimental.pallas import tpu as pltpu
from jax.sharding import Mesh, PartitionSpec as P

HS = 128
HOPS = 4
CAP = 3
VMEM_GRANT = 56 * 2**20
BF = jnp.bfloat16
F16 = jnp.float16
F32 = jnp.float32
X = ("xh", "xl")
EP = ("xh", "xl", "z", "core")
XC = ("xh", "xl", "core")
XZ = ("xh", "xl", "z")
ZC = ("z", "core")


def from_earlier(value, by):
    chips = lax.axis_size(XZ)
    return lax.ppermute(value, XZ, [(i, i + by) for i in range(chips - by)])


def shift(value, axis, by):
    devices = lax.axis_size(axis)
    return lax.ppermute(value, axis, [(i, (i + by) % devices) for i in range(devices)])


def contract(left, right, dims):
    return lax.dot_general(left, right, (dims, ((), ())), preferred_element_type=F32)


def attention(queries, keys, values, doc_start):
    tok_ep = queries.shape[0]
    group_size = queries.shape[1] // HS
    cores = lax.axis_size("core")
    chips = -(-HOPS // cores)
    own = lax.all_gather(jnp.concatenate([keys, values], 1), "core", axis=0, tiled=True)
    both = jnp.concatenate([from_earlier(own, by) for by in range(chips, 0, -1)] + [own], 0)
    key_all, value_all = both[:, :HS], both[:, HS:]
    first = (lax.axis_index(XZ) - chips) * cores * tok_ep
    key_pos = first + jnp.arange(both.shape[0], dtype=jnp.int32)
    query_pos = lax.axis_index(EP) * tok_ep + jnp.arange(tok_ep, dtype=jnp.int32)
    key_mask = (key_pos[None, :] <= query_pos[:, None]) & (key_pos[None, :] >= doc_start[:, None])
    query_heads = queries.reshape(tok_ep, group_size, HS)
    score_vals = jnp.einsum("igd,jd->gij", query_heads, key_all, preferred_element_type=F32) * (
        1.0 / HS**0.5
    )
    score_vals = jnp.where(key_mask[None], score_vals, -jnp.inf)
    row_peak = jnp.max(score_vals, axis=-1, keepdims=True)
    prob_vals = jnp.exp(score_vals - row_peak)
    row_total = jnp.sum(prob_vals, axis=-1, keepdims=True)
    weighted = jnp.einsum("gij,jd->igd", prob_vals.astype(BF), value_all, preferred_element_type=F32)
    return (
        (weighted / jnp.transpose(row_total, (1, 0, 2))).reshape(tok_ep, group_size * HS).astype(BF)
    )


def slot_ranks(ids, experts, core_of):
    match = ids[None] == experts[:, None, None]
    hit = jnp.any(match, axis=1)
    step = jnp.arange(ids.shape[1], dtype=jnp.int32)
    before = (step[:, None] < step[None, :]) & (core_of[:, None] == core_of[None, :])
    rank = jnp.dot(hit.astype(BF), before.astype(BF), preferred_element_type=F32).astype(jnp.int32)
    return match, jnp.where(hit, rank, -1)


def expert_kernel(chunk, rows_ref, gate_ref, up_ref, down_ref, *refs):
    out_ref, gate_vm, up_vm, down_vm, hidden_ref, sems = refs
    units, parts = gate_ref.shape[0], down_ref.shape[0]
    cols = down_ref.shape[2]
    steps = units // chunk
    copies = []
    for step in range(steps):
        at = pl.ds(step * chunk, chunk)
        copies.append((gate_ref.at[at], gate_vm.at[at]))
        copies.append((up_ref.at[at], up_vm.at[at]))
    for part in range(parts):
        copies.append((down_ref.at[part], down_vm.at[part]))
    copies = [pltpu.make_async_copy(*pair, sems.at[i]) for i, pair in enumerate(copies)]
    for copy in copies:
        copy.start()
    rows = rows_ref[...]
    for step in range(steps):
        copies[2 * step].wait()
        copies[2 * step + 1].wait()
        at = slice(step * chunk, (step + 1) * chunk)
        gate = contract(rows, gate_vm[at], ((1,), (1,)))
        up = contract(rows, up_vm[at], ((1,), (1,)))
        hidden_ref[:, at] = (gate / (1.0 + jnp.exp(-gate)) * up).astype(BF)
    hidden = hidden_ref[...]
    for part in range(parts):
        copies[2 * steps + part].wait()
        total = jnp.dot(hidden, down_vm[part], preferred_element_type=F32)
        out_ref[:, part * cols : (part + 1) * cols] = total.astype(BF)


def expert(rows, gate, up, down, parts):
    count, width = rows.shape
    down = down.reshape(parts, -1, down.shape[1])
    chunk = min(256, gate.shape[0])
    vmem, hbm = pl.BlockSpec(memory_space=pltpu.VMEM), pl.BlockSpec(memory_space=pltpu.HBM)
    return pl.pallas_call(
        functools.partial(expert_kernel, chunk),
        in_specs=[vmem, hbm, hbm, hbm],
        out_specs=vmem,
        out_shape=jax.ShapeDtypeStruct((count, width), BF),
        scratch_shapes=[
            pltpu.VMEM(gate.shape, BF),
            pltpu.VMEM(up.shape, BF),
            pltpu.VMEM(down.shape, BF),
            pltpu.VMEM((count, gate.shape[0]), BF),
            pltpu.SemaphoreType.DMA((2 * (gate.shape[0] // chunk) + parts,)),
        ],
        compiler_params=pltpu.CompilerParams(vmem_limit_bytes=VMEM_GRANT),
        cost_estimate=pl.CostEstimate(
            flops=2 * count * (gate.size + up.size + down.size),
            bytes_accessed=2 * (2 * rows.size + gate.size + up.size + down.size),
            transcendentals=count * gate.shape[0],
        ),
    )(rows, gate, up, down)


def add_low(left, right):
    return (left.astype(F32) + right.astype(F32)).astype(BF)


def ring_sums(chunks):
    places = len(chunks)

    def two(k):
        return jnp.concatenate([chunks[k % places], chunks[(k - 1) % places]], 0)

    def two_back(k):
        return jnp.concatenate([chunks[-k % places], chunks[(1 - k) % places]], 0)

    rows = chunks[0].shape[0]
    half = places // 2
    right, left = two(half), two_back(half - 1)
    for k in range(half - 2, 0, -2):
        right = add_low(shift(right, "z", 2), two(k))
        left = shift(left, "z", -2)
        if k > 2:
            left = add_low(left, two_back(k - 1))
    last = shift(add_low(left[:rows], chunks[-1]), "z", -1)
    pieces = [left[rows:], shift(right[:rows], "z", 2), shift(right[rows:], "z", 1), last]
    return sum((p.astype(F32) for p in pieces), chunks[0].astype(F32))


def on_device(
    queries,
    keys,
    values,
    doc_start,
    residual,
    out_weight,
    norm_gain,
    gate_weight,
    up_weight,
    down_weight,
    route_ids,
    route_weights,
):
    nx, nz, nc, nr = (lax.axis_size(a) for a in (X, "z", "core", "rep"))
    width = out_weight.shape[1]
    rows8 = out_weight.shape[0]
    tok_sub, top = route_ids.shape[1], route_ids.shape[2]
    here = lax.axis_index("z")

    gate_all = lax.all_gather(gate_weight[0], "rep", axis=0, tiled=True)
    up_all = lax.all_gather(up_weight[0], "rep", axis=0, tiled=True)
    down_all = lax.all_gather(down_weight[0], "rep", axis=0, tiled=True)

    own_rows = out_weight.astype(F16)
    pair_rows = jnp.concatenate([own_rows, shift(own_rows, "xl", 1)], 0)
    info = jnp.concatenate([route_ids[0].astype(F16), route_weights[0].astype(F16)], 1)
    info = jnp.pad(info, ((0, 0), (0, 128 - 2 * top)))
    groups = tok_sub // (2 * rows8)
    info = [info[g * 2 * rows8 : (g + 1) * 2 * rows8] for g in range(groups)]
    pair_rows = jnp.concatenate([pair_rows] + info, 1)

    attended = attention(queries, keys, values, doc_start)
    half = attended.shape[1] // 2
    xh = lax.axis_index("xh")
    low, high = attended[:, :half], attended[:, half:]
    kept = jnp.where(xh == 0, low, high)
    given = jnp.where(xh == 0, high, low)
    got = shift(given, "xh", 1)
    pair_rows, _ = lax.optimization_barrier((pair_rows, given))
    z_all = lax.all_gather(pair_rows, ZC, axis=0, tiled=True)
    out_rows = z_all[:, :width].astype(BF)

    both = jnp.stack([jnp.where(xh == 0, kept, got), jnp.where(xh == 0, got, kept)], 0)
    both = both.reshape(2, nr, tok_sub, half).transpose(1, 0, 2, 3).reshape(-1, half)
    place = jnp.arange(half, dtype=jnp.int32)
    pi, px = place % rows8, place // rows8 % 2
    px = jnp.where(lax.axis_index("xl") == 0, px, 1 - px)
    pc, pz = place // (2 * rows8) % nc, place // (2 * rows8 * nc)
    source = ((px * nz + pz) * nc + pc) * rows8 + pi
    permute = (place[:, None] == source[None, :]).astype(BF)
    both = jnp.dot(both, permute, preferred_element_type=F32).astype(BF)
    partial_value = jnp.dot(both, out_rows, preferred_element_type=F32).astype(BF)
    parts = lax.all_to_all(partial_value, ("rep", "xh"), split_axis=0, concat_axis=0, tiled=True)
    head_total = jnp.sum(parts.reshape(-1, tok_sub, width).astype(F32), axis=0)
    hidden_sum = residual[0].astype(F32) + head_total
    inverse_rms = lax.rsqrt(jnp.mean(hidden_sum * hidden_sum, axis=-1, keepdims=True) + 1e-06)
    normed = (hidden_sum * inverse_rms * norm_gain).astype(BF)
    column = lax.all_gather(normed.astype(F16), ZC, axis=0, tiled=True).astype(BF)

    table = [z_all[:, width + 128 * g :][:, : 2 * top].astype(F32) for g in range(groups)]
    table = jnp.stack([jnp.transpose(t).reshape(2 * top, -1, 2 * rows8) for t in table], 2)
    table = table.reshape(2 * top, -1)
    count = table.shape[1]
    core = lax.axis_index("core")
    core_of = jnp.arange(count, dtype=jnp.int32) // tok_sub % nc
    slot = jnp.arange(CAP * nz, dtype=jnp.int32)
    ids = table[:top].astype(jnp.int32)
    experts = (jnp.arange(nx, dtype=jnp.int32) * nz + here) * nc + core
    _, rank = slot_ranks(ids, experts, core_of)
    seat = core_of[None, :] * slot.size + rank
    seat = jnp.where(rank < 0, -1, seat)
    seats = jnp.arange(nc * slot.size, dtype=jnp.int32)
    send = (seat[:, None, :] == seats[None, :, None]).astype(BF).reshape(-1, count)

    table = table.reshape(2 * top, nz, nc, tok_sub)
    table = lax.dynamic_slice_in_dim(table, core, 1, 2).reshape(2 * top, -1)
    lane = jnp.arange(nx * nc, dtype=jnp.int32)
    experts = ((lane // nc) * nz + here) * nc + lane % nc
    own_count = table.shape[1]
    match, rank = slot_ranks(
        table[:top].astype(jnp.int32), experts, jnp.zeros((own_count,), jnp.int32)
    )
    gain = jnp.sum(jnp.where(match, table[None, top:], 0.0), axis=1)

    def back_for(rank, gain):
        back = jnp.where(rank[:, None, :] == slot[None, :, None], gain[:, None, :], 0.0)
        return back.astype(BF).reshape(-1, own_count)

    def from_here(value):
        value = value.reshape(-1, nz, tok_sub)
        value = lax.dynamic_slice_in_dim(jnp.concatenate([value, value], 1), here, nz, 1)
        return value.reshape(-1, own_count)

    back = back_for(from_here(rank), from_here(gain))

    send_rows = jnp.dot(send, column, preferred_element_type=F32).astype(BF)
    rows = lax.all_to_all(send_rows, X, split_axis=0, concat_axis=0, tiled=True)
    expert_out = expert(rows, gate_all, up_all, down_all, nr)
    returned = lax.all_to_all(expert_out, XC, split_axis=0, concat_axis=0, tiled=True)
    mixed = contract(back, returned, ((0,), (0,))).astype(BF)
    expert_mix = ring_sums([mixed[k * tok_sub : (k + 1) * tok_sub] for k in range(nz)])
    return (hidden_sum + expert_mix).astype(BF)[None]


def solution(mesh):
    devices = mesh.devices
    split = Mesh(devices.reshape(4, 2, 2, devices.shape[1] // 8, 2), ("rep",) + EP)
    placed = (
        P(EP, "rep"),
        P(EP, "rep"),
        P(EP, "rep"),
        P(EP),
        P(EP, "rep", None),
        P(("rep",) + EP, None),
        P(),
        P(EP, "rep", None),
        P(EP, "rep", None),
        P(EP, None, "rep"),
        P(EP, "rep", None),
        P(EP, "rep", None),
    )
    return jax.shard_map(
        on_device, mesh=split, in_specs=placed, out_specs=P(EP, "rep", None), check_vma=False
    )
```

```python
import functools

import jax
import jax.numpy as jnp
from jax import lax
from jax.experimental import pallas as pl
from jax.experimental.pallas import tpu as pltpu
from jax.sharding import Mesh, PartitionSpec as P

HS = 128
HOPS = 4
CAP = 3
VMEM_GRANT = 56 * 2**20
BF = jnp.bfloat16
F16 = jnp.float16
F32 = jnp.float32
X = ("xh", "xl")
EP = ("xh", "xl", "z", "core")
XC = ("xh", "xl", "core")
XZ = ("xh", "xl", "z")
ZC = ("z", "core")


def from_earlier(value, by):
    chips = lax.axis_size(XZ)
    return lax.ppermute(value, XZ, [(i, i + by) for i in range(chips - by)])


def shift(value, axis, by):
    devices = lax.axis_size(axis)
    return lax.ppermute(value, axis, [(i, (i + by) % devices) for i in range(devices)])


def contract(left, right, dims):
    return lax.dot_general(left, right, (dims, ((), ())), preferred_element_type=F32)


def attention(queries, keys, values, doc_start):
    tok_ep = queries.shape[0]
    group_size = queries.shape[1] // HS
    cores = lax.axis_size("core")
    chips = -(-HOPS // cores)
    own = lax.all_gather(jnp.concatenate([keys, values], 1), "core", axis=0, tiled=True)
    both = jnp.concatenate([from_earlier(own, by) for by in range(chips, 0, -1)] + [own], 0)
    key_all, value_all = both[:, :HS], both[:, HS:]
    first = (lax.axis_index(XZ) - chips) * cores * tok_ep
    key_pos = first + jnp.arange(both.shape[0], dtype=jnp.int32)
    query_pos = lax.axis_index(EP) * tok_ep + jnp.arange(tok_ep, dtype=jnp.int32)
    key_mask = (key_pos[None, :] <= query_pos[:, None]) & (key_pos[None, :] >= doc_start[:, None])
    query_heads = queries.reshape(tok_ep, group_size, HS)
    score_vals = jnp.einsum("igd,jd->gij", query_heads, key_all, preferred_element_type=F32) * (
        1.0 / HS**0.5
    )
    score_vals = jnp.where(key_mask[None], score_vals, -jnp.inf)
    row_peak = jnp.max(score_vals, axis=-1, keepdims=True)
    prob_vals = jnp.exp(score_vals - row_peak)
    row_total = jnp.sum(prob_vals, axis=-1, keepdims=True)
    weighted = jnp.einsum("gij,jd->igd", prob_vals.astype(BF), value_all, preferred_element_type=F32)
    return (
        (weighted / jnp.transpose(row_total, (1, 0, 2))).reshape(tok_ep, group_size * HS).astype(BF)
    )


def slot_ranks(ids, experts, class_of):
    match = ids[None] == experts[:, None, None]
    hit = jnp.any(match, axis=1)
    step = jnp.arange(ids.shape[1], dtype=jnp.int32)
    before = (step[:, None] < step[None, :]) & (class_of[:, None] == class_of[None, :])
    rank = jnp.dot(hit.astype(BF), before.astype(BF), preferred_element_type=F32).astype(jnp.int32)
    return match, jnp.where(hit, rank, -1)


def expert_kernel(chunk, group, rows_ref, gate_ref, up_ref, down_ref, *refs):
    far_ref, near_ref, gate_vm, up_vm, down_vm, hidden_ref, sems = refs
    units, parts = gate_ref.shape[0], down_ref.shape[0]
    cols = down_ref.shape[2]
    steps = units // chunk
    copies = []
    for step in range(steps):
        at = pl.ds(step * chunk, chunk)
        copies.append((gate_ref.at[at], gate_vm.at[at]))
        copies.append((up_ref.at[at], up_vm.at[at]))
    for part in range(parts):
        copies.append((down_ref.at[part], down_vm.at[part]))
    copies = [pltpu.make_async_copy(*pair, sems.at[i]) for i, pair in enumerate(copies)]
    ahead = 4
    for copy in copies[:ahead]:
        copy.start()

    def arrived(i):
        copies[i].wait()
        if i + ahead < len(copies):
            copies[i + ahead].start()

    rows = rows_ref[...]
    for step in range(steps):
        arrived(2 * step)
        arrived(2 * step + 1)
        at = slice(step * chunk, (step + 1) * chunk)
        gate = contract(rows, gate_vm[at], ((1,), (1,)))
        up = contract(rows, up_vm[at], ((1,), (1,)))
        hidden_ref[:, at] = (gate / (1.0 + jnp.exp(-gate)) * up).astype(BF)
    hidden = hidden_ref[...]
    for part in range(parts):
        arrived(2 * steps + part)
        total = jnp.dot(hidden, down_vm[part], preferred_element_type=F32).astype(BF)
        at = slice(part * cols, (part + 1) * cols)
        for k in range(far_ref.shape[0] // group):
            begin = 2 * k * group
            far_ref[k * group : (k + 1) * group, at] = total[begin : begin + group]
            near_ref[k * group : (k + 1) * group, at] = total[begin + group : begin + 2 * group]


def expert(rows, gate, up, down, parts, group):
    count, width = rows.shape
    down = down.reshape(parts, -1, down.shape[1])
    chunk = min(256, gate.shape[0])
    vmem, hbm = pl.BlockSpec(memory_space=pltpu.VMEM), pl.BlockSpec(memory_space=pltpu.HBM)
    return pl.pallas_call(
        functools.partial(expert_kernel, chunk, group),
        in_specs=[vmem, hbm, hbm, hbm],
        out_specs=[vmem, vmem],
        out_shape=[jax.ShapeDtypeStruct((count // 2, width), BF)] * 2,
        scratch_shapes=[
            pltpu.VMEM(gate.shape, BF),
            pltpu.VMEM(up.shape, BF),
            pltpu.VMEM(down.shape, BF),
            pltpu.VMEM((count, gate.shape[0]), BF),
            pltpu.SemaphoreType.DMA((2 * (gate.shape[0] // chunk) + parts,)),
        ],
        compiler_params=pltpu.CompilerParams(vmem_limit_bytes=VMEM_GRANT),
        cost_estimate=pl.CostEstimate(
            flops=2 * count * (gate.size + up.size + down.size),
            bytes_accessed=2 * (2 * rows.size + gate.size + up.size + down.size),
            transcendentals=count * gate.shape[0],
        ),
    )(rows, gate, up, down)


def add_low(left, right):
    return (left.astype(F32) + right.astype(F32)).astype(BF)


def pair_up(chunks, k):
    places = len(chunks)
    return jnp.concatenate([chunks[k % places], chunks[(k - 1) % places]], 0)


def pair_down(chunks, k):
    places = len(chunks)
    return jnp.concatenate([chunks[-k % places], chunks[(1 - k) % places]], 0)


def ring_sums(chunks, right, left):
    half = len(chunks) // 2
    rows = chunks[0].shape[0]
    for k in range(half - 2, 0, -2):
        right = add_low(shift(right, "z", 2), pair_up(chunks, k))
        left = shift(left, "z", -2)
        if k > 2:
            left = add_low(left, pair_down(chunks, k - 1))
    last = shift(add_low(left[:rows], chunks[-1]), "z", -1)
    pieces = [left[rows:], shift(right[:rows], "z", 2), shift(right[rows:], "z", 1), last]
    return sum((p.astype(F32) for p in pieces), chunks[0].astype(F32))


def on_device(
    queries,
    keys,
    values,
    doc_start,
    residual,
    out_weight,
    norm_gain,
    gate_weight,
    up_weight,
    down_weight,
    route_ids,
    route_weights,
):
    nx, nz, nc, nr = (lax.axis_size(a) for a in (X, "z", "core", "rep"))
    width = out_weight.shape[1]
    rows8 = out_weight.shape[0]
    tok_sub, top = route_ids.shape[1], route_ids.shape[2]
    here = lax.axis_index("z")

    gate_all = lax.all_gather(gate_weight[0], "rep", axis=0, tiled=True)
    up_all = lax.all_gather(up_weight[0], "rep", axis=0, tiled=True)
    down_all = lax.all_gather(down_weight[0], "rep", axis=0, tiled=True)

    own_rows = out_weight.astype(F16)
    pair_rows = jnp.concatenate([own_rows, shift(own_rows, "xl", 1)], 0)
    info = jnp.concatenate([route_ids[0].astype(F16), route_weights[0].astype(F16)], 1)
    info = jnp.pad(info, ((0, 0), (0, 128 - 2 * top)))
    groups = tok_sub // (2 * rows8)
    info = [info[g * 2 * rows8 : (g + 1) * 2 * rows8] for g in range(groups)]
    pair_rows = jnp.concatenate([pair_rows] + info, 1)

    attended = attention(queries, keys, values, doc_start)
    half = attended.shape[1] // 2
    xh = lax.axis_index("xh")
    low, high = attended[:, :half], attended[:, half:]
    kept = jnp.where(xh == 0, low, high)
    given = jnp.where(xh == 0, high, low)
    got = shift(given, "xh", 1)
    pair_rows, _ = lax.optimization_barrier((pair_rows, given))
    z_all = lax.all_gather(pair_rows, ZC, axis=0, tiled=True)
    out_rows = z_all[:, :width].astype(BF)

    both = jnp.stack([jnp.where(xh == 0, kept, got), jnp.where(xh == 0, got, kept)], 0)
    both = both.reshape(2, nr, tok_sub, half).transpose(1, 0, 2, 3).reshape(-1, half)
    place = jnp.arange(half, dtype=jnp.int32)
    pi, px = place % rows8, place // rows8 % 2
    px = jnp.where(lax.axis_index("xl") == 0, px, 1 - px)
    pc, pz = place // (2 * rows8) % nc, place // (2 * rows8 * nc)
    source = ((px * nz + pz) * nc + pc) * rows8 + pi
    permute = (place[:, None] == source[None, :]).astype(BF)
    both = jnp.dot(both, permute, preferred_element_type=F32).astype(BF)
    partial_value = jnp.dot(both, out_rows, preferred_element_type=F32).astype(BF)
    parts = lax.all_to_all(partial_value, ("rep", "xh"), split_axis=0, concat_axis=0, tiled=True)
    head_total = jnp.sum(parts.reshape(-1, tok_sub, width).astype(F32), axis=0)
    hidden_sum = residual[0].astype(F32) + head_total
    inverse_rms = lax.rsqrt(jnp.mean(hidden_sum * hidden_sum, axis=-1, keepdims=True) + 1e-06)
    normed = (hidden_sum * inverse_rms * norm_gain).astype(BF)
    column = lax.all_gather(normed.astype(F16), ZC, axis=0, tiled=True).astype(BF)

    table = [z_all[:, width + 128 * g :][:, : 2 * top].astype(F32) for g in range(groups)]
    table = jnp.stack([jnp.transpose(t).reshape(2 * top, -1, 2 * rows8) for t in table], 2)
    table = table.reshape(2 * top, -1)
    count = table.shape[1]
    core = lax.axis_index("core")
    lanes = jnp.arange(count, dtype=jnp.int32)
    core_of = lanes // tok_sub % nc
    near_places = list(range(nz - nz // 4 + 1, nz)) + list(range(nz // 4 + 1))
    far_places = list(range(nz // 4 + 1, nz - nz // 4 + 1))
    cap = CAP * nz // 2

    def is_near(place):
        offset = (place - here + nz) % nz
        return ((offset <= nz // 4) | (offset > nz - nz // 4)).astype(jnp.int32)

    near = is_near(lanes // (tok_sub * nc))
    ids = table[:top].astype(jnp.int32)
    experts = (jnp.arange(nx, dtype=jnp.int32) * nz + here) * nc + core
    _, rank = slot_ranks(ids, experts, near * nc + core_of)
    seat = (near * nc + core_of)[None, :] * cap + rank
    seat = jnp.where(rank < 0, -1, seat)
    seats = jnp.arange(2 * nc * cap, dtype=jnp.int32)
    send = (seat[:, None, :] == seats[None, :, None]).astype(BF).reshape(-1, count)

    table = table.reshape(2 * top, nz, nc, tok_sub)
    table = lax.dynamic_slice_in_dim(table, core, 1, 2).reshape(2 * top, -1)
    lane = jnp.arange(nx * nc, dtype=jnp.int32)
    experts = ((lane // nc) * nz + here) * nc + lane % nc
    own_count = table.shape[1]
    match, rank = slot_ranks(
        table[:top].astype(jnp.int32),
        experts,
        is_near(jnp.arange(own_count, dtype=jnp.int32) // tok_sub),
    )
    gain = jnp.sum(jnp.where(match, table[None, top:], 0.0), axis=1)

    def blocks_of(value, places):
        value = value.reshape(-1, nz, tok_sub)
        value = lax.dynamic_slice_in_dim(jnp.concatenate([value, value], 1), here, nz, 1)
        return jnp.concatenate([value[:, k] for k in places], 1)

    def back_for(places):
        slot = jnp.arange(cap, dtype=jnp.int32)
        taken = blocks_of(rank, places)[:, None, :] == slot[None, :, None]
        back = jnp.where(taken, blocks_of(gain, places)[:, None, :], 0.0)
        return back.astype(BF).reshape(len(experts) * cap, -1)

    backs = back_for(far_places), back_for(near_places)

    send_rows = jnp.dot(send, column, preferred_element_type=F32).astype(BF)
    rows = lax.all_to_all(send_rows, X, split_axis=0, concat_axis=0, tiled=True)
    far, near = expert(rows, gate_all, up_all, down_all, nr, nc * cap)
    chunks = [None] * nz

    def spread_out(out, back, places):
        returned = lax.all_to_all(out, XC, split_axis=0, concat_axis=0, tiled=True)
        mixed = contract(back, returned, ((0,), (0,))).astype(BF)
        for i, place in enumerate(places):
            chunks[place] = mixed[i * tok_sub : (i + 1) * tok_sub]

    spread_out(far, backs[0], far_places)
    right, left = pair_up(chunks, nz // 2), pair_down(chunks, nz // 2 - 1)
    right, left, near = lax.optimization_barrier((right, left, near))
    spread_out(near, backs[1], near_places)
    expert_mix = ring_sums(chunks, right, left)
    return (hidden_sum + expert_mix).astype(BF)[None]


def solution(mesh):
    devices = mesh.devices
    split = Mesh(devices.reshape(4, 2, 2, devices.shape[1] // 8, 2), ("rep",) + EP)
    placed = (
        P(EP, "rep"),
        P(EP, "rep"),
        P(EP, "rep"),
        P(EP),
        P(EP, "rep", None),
        P(("rep",) + EP, None),
        P(),
        P(EP, "rep", None),
        P(EP, "rep", None),
        P(EP, None, "rep"),
        P(EP, "rep", None),
        P(EP, "rep", None),
    )
    return jax.shard_map(
        on_device, mesh=split, in_specs=placed, out_specs=P(EP, "rep", None), check_vma=False
    )
```

```python
import functools

import jax
import jax.numpy as jnp
from jax import lax
from jax.experimental import pallas as pl
from jax.experimental.pallas import tpu as pltpu
from jax.sharding import Mesh, PartitionSpec as P

HS = 128
HOPS = 4
CAP = 3
VMEM_GRANT = 56 * 2**20
WEIGHT_SCALE = 2.0**19
ROW_SCALE = 2.0**9
BF = jnp.bfloat16
F16 = jnp.float16
F32 = jnp.float32
X = ("xh", "xl")
EP = ("xh", "xl", "z", "core")
XC = ("xh", "xl", "core")
XZ = ("xh", "xl", "z")
ZC = ("z", "core")


def from_earlier(value, by):
    chips = lax.axis_size(XZ)
    return lax.ppermute(value, XZ, [(i, i + by) for i in range(chips - by)])


def shift(value, axis, by):
    devices = lax.axis_size(axis)
    return lax.ppermute(value, axis, [(i, (i + by) % devices) for i in range(devices)])


def contract(left, right, dims):
    return lax.dot_general(left, right, (dims, ((), ())), preferred_element_type=F32)


def attention(queries, keys, values, doc_start):
    tok_ep = queries.shape[0]
    group_size = queries.shape[1] // HS
    cores = lax.axis_size("core")
    chips = -(-HOPS // cores)
    own = lax.all_gather(jnp.concatenate([keys, values], 1), "core", axis=0, tiled=True)
    both = jnp.concatenate([from_earlier(own, by) for by in range(chips, 0, -1)] + [own], 0)
    key_all, value_all = both[:, :HS], both[:, HS:]
    first = (lax.axis_index(XZ) - chips) * cores * tok_ep
    key_pos = first + jnp.arange(both.shape[0], dtype=jnp.int32)
    query_pos = lax.axis_index(EP) * tok_ep + jnp.arange(tok_ep, dtype=jnp.int32)
    key_mask = (key_pos[None, :] <= query_pos[:, None]) & (key_pos[None, :] >= doc_start[:, None])
    query_heads = queries.reshape(tok_ep, group_size, HS)
    score_vals = jnp.einsum("igd,jd->gij", query_heads, key_all, preferred_element_type=F32) * (
        1.0 / HS**0.5
    )
    score_vals = jnp.where(key_mask[None], score_vals, -jnp.inf)
    row_peak = jnp.max(score_vals, axis=-1, keepdims=True)
    prob_vals = jnp.exp(score_vals - row_peak)
    row_total = jnp.sum(prob_vals, axis=-1, keepdims=True)
    weighted = jnp.einsum("gij,jd->igd", prob_vals.astype(BF), value_all, preferred_element_type=F32)
    return (
        (weighted / jnp.transpose(row_total, (1, 0, 2))).reshape(tok_ep, group_size * HS).astype(BF)
    )


def slot_ranks(ids, experts, class_of):
    match = ids[None] == experts[:, None, None]
    hit = jnp.any(match, axis=1)
    step = jnp.arange(ids.shape[1], dtype=jnp.int32)
    before = (step[:, None] < step[None, :]) & (class_of[:, None] == class_of[None, :])
    rank = jnp.dot(hit.astype(BF), before.astype(BF), preferred_element_type=F32).astype(jnp.int32)
    return match, jnp.where(hit, rank, -1)


def expert_kernel(chunk, group, rows_ref, gate_ref, up_ref, down_ref, *refs):
    far_ref, near_ref, gate_vm, up_vm, down_vm, hidden_ref, sems = refs
    units, parts = gate_ref.shape[0], down_ref.shape[0]
    cols = down_ref.shape[2]
    steps = units // chunk
    copies = []
    for step in range(steps):
        at = pl.ds(step * chunk, chunk)
        copies.append((gate_ref.at[at], gate_vm.at[at]))
        copies.append((up_ref.at[at], up_vm.at[at]))
    for part in range(parts):
        copies.append((down_ref.at[part], down_vm.at[part]))
    copies = [pltpu.make_async_copy(*pair, sems.at[i]) for i, pair in enumerate(copies)]
    ahead = 4
    for copy in copies[:ahead]:
        copy.start()

    def arrived(i):
        copies[i].wait()
        if i + ahead < len(copies):
            copies[i + ahead].start()

    rows = rows_ref[...]
    for step in range(steps):
        arrived(2 * step)
        arrived(2 * step + 1)
        at = slice(step * chunk, (step + 1) * chunk)
        gate = contract(rows, gate_vm[at], ((1,), (1,)))
        up = contract(rows, up_vm[at], ((1,), (1,)))
        hidden_ref[:, at] = (gate / (1.0 + jnp.exp(-gate)) * up).astype(BF)
    hidden = hidden_ref[...]
    for part in range(parts):
        arrived(2 * steps + part)
        total = jnp.dot(hidden, down_vm[part], preferred_element_type=F32).astype(BF)
        at = slice(part * cols, (part + 1) * cols)
        for k in range(far_ref.shape[0] // group):
            begin = 2 * k * group
            far_ref[k * group : (k + 1) * group, at] = total[begin : begin + group]
            near_ref[k * group : (k + 1) * group, at] = total[begin + group : begin + 2 * group]


def expert(rows, gate, up, down, parts, group):
    count, width = rows.shape
    down = down.reshape(parts, -1, down.shape[1])
    chunk = min(256, gate.shape[0])
    vmem, hbm = pl.BlockSpec(memory_space=pltpu.VMEM), pl.BlockSpec(memory_space=pltpu.HBM)
    return pl.pallas_call(
        functools.partial(expert_kernel, chunk, group),
        in_specs=[vmem, hbm, hbm, hbm],
        out_specs=[vmem, vmem],
        out_shape=[jax.ShapeDtypeStruct((count // 2, width), BF)] * 2,
        scratch_shapes=[
            pltpu.VMEM(gate.shape, BF),
            pltpu.VMEM(up.shape, BF),
            pltpu.VMEM(down.shape, BF),
            pltpu.VMEM((count, gate.shape[0]), BF),
            pltpu.SemaphoreType.DMA((2 * (gate.shape[0] // chunk) + parts,)),
        ],
        compiler_params=pltpu.CompilerParams(vmem_limit_bytes=VMEM_GRANT),
        cost_estimate=pl.CostEstimate(
            flops=2 * count * (gate.size + up.size + down.size),
            bytes_accessed=2 * (2 * rows.size + gate.size + up.size + down.size),
            transcendentals=count * gate.shape[0],
        ),
    )(rows, gate, up, down)


def add_low(left, right):
    return (left.astype(F32) + right.astype(F32)).astype(BF)


def pair_up(chunks, k):
    places = len(chunks)
    return jnp.concatenate([chunks[k % places], chunks[(k - 1) % places]], 0)


def pair_down(chunks, k):
    places = len(chunks)
    return jnp.concatenate([chunks[-k % places], chunks[(1 - k) % places]], 0)


def ring_sums(chunks, right, left):
    half = len(chunks) // 2
    rows = chunks[0].shape[0]
    for k in range(half - 2, 0, -2):
        right = add_low(shift(right, "z", 2), pair_up(chunks, k))
        left = shift(left, "z", -2)
        if k > 2:
            left = add_low(left, pair_down(chunks, k - 1))
    last = shift(add_low(left[:rows], chunks[-1]), "z", -1)
    pieces = [left[rows:], shift(right[:rows], "z", 2), shift(right[rows:], "z", 1), last]
    return sum((p.astype(F32) for p in pieces), chunks[0].astype(F32))


def on_device(
    queries,
    keys,
    values,
    doc_start,
    residual,
    out_weight,
    norm_gain,
    gate_weight,
    up_weight,
    down_weight,
    route_ids,
    route_weights,
):
    nx, nz, nc, nr = (lax.axis_size(a) for a in (X, "z", "core", "rep"))
    width = out_weight.shape[1]
    rows8 = out_weight.shape[0]
    tok_sub, top = route_ids.shape[1], route_ids.shape[2]
    here = lax.axis_index("z")

    gate_all = lax.all_gather(gate_weight[0], "rep", axis=0, tiled=True)
    up_all = lax.all_gather(up_weight[0], "rep", axis=0, tiled=True)
    down_all = lax.all_gather(down_weight[0], "rep", axis=0, tiled=True)

    own_rows = (out_weight * WEIGHT_SCALE).astype(F16)
    pair_rows = jnp.concatenate([own_rows, shift(own_rows, "xl", 1)], 0)
    info = jnp.concatenate([route_ids[0].astype(F16), route_weights[0].astype(F16)], 1)
    info = jnp.pad(info, ((0, 0), (0, 128 - 2 * top)))
    groups = tok_sub // (2 * rows8)
    info = [info[g * 2 * rows8 : (g + 1) * 2 * rows8] for g in range(groups)]
    pair_rows = jnp.concatenate([pair_rows] + info, 1)

    attended = attention(queries, keys, values, doc_start)
    half = attended.shape[1] // 2
    xh = lax.axis_index("xh")
    low, high = attended[:, :half], attended[:, half:]
    kept = jnp.where(xh == 0, low, high)
    given = jnp.where(xh == 0, high, low)
    got = shift(given, "xh", 1)
    pair_rows, _ = lax.optimization_barrier((pair_rows, given))
    z_all = lax.all_gather(pair_rows, ZC, axis=0, tiled=True)
    out_rows = z_all[:, :width].astype(BF)

    both = jnp.stack([jnp.where(xh == 0, kept, got), jnp.where(xh == 0, got, kept)], 0)
    both = both.reshape(2, nr, tok_sub, half).transpose(1, 0, 2, 3).reshape(-1, half)
    place = jnp.arange(half, dtype=jnp.int32)
    pi, px = place % rows8, place // rows8 % 2
    px = jnp.where(lax.axis_index("xl") == 0, px, 1 - px)
    pc, pz = place // (2 * rows8) % nc, place // (2 * rows8 * nc)
    source = ((px * nz + pz) * nc + pc) * rows8 + pi
    permute = (place[:, None] == source[None, :]).astype(BF)
    both = jnp.dot(both, permute, preferred_element_type=F32).astype(BF)
    partial_value = jnp.dot(both, out_rows, preferred_element_type=F32)
    partial_value = (partial_value * (1.0 / WEIGHT_SCALE)).astype(BF)
    parts = lax.all_to_all(partial_value, ("rep", "xh"), split_axis=0, concat_axis=0, tiled=True)
    head_total = jnp.sum(parts.reshape(-1, tok_sub, width).astype(F32), axis=0)
    hidden_sum = residual[0].astype(F32) + head_total
    inverse_rms = lax.rsqrt(jnp.mean(hidden_sum * hidden_sum, axis=-1, keepdims=True) + 1e-06)
    normed = (hidden_sum * inverse_rms * norm_gain).astype(BF)
    column = (normed * ROW_SCALE).astype(F16)
    column = lax.all_gather(column, ZC, axis=0, tiled=True).astype(BF)

    table = [z_all[:, width + 128 * g :][:, : 2 * top].astype(F32) for g in range(groups)]
    table = jnp.stack([jnp.transpose(t).reshape(2 * top, -1, 2 * rows8) for t in table], 2)
    table = table.reshape(2 * top, -1)
    count = table.shape[1]
    core = lax.axis_index("core")
    lanes = jnp.arange(count, dtype=jnp.int32)
    core_of = lanes // tok_sub % nc
    near_places = list(range(nz - nz // 4 + 1, nz)) + list(range(nz // 4 + 1))
    far_places = list(range(nz // 4 + 1, nz - nz // 4 + 1))
    cap = CAP * nz // 2

    def is_near(place):
        offset = (place - here + nz) % nz
        return ((offset <= nz // 4) | (offset > nz - nz // 4)).astype(jnp.int32)

    near = is_near(lanes // (tok_sub * nc))
    ids = table[:top].astype(jnp.int32)
    experts = (jnp.arange(nx, dtype=jnp.int32) * nz + here) * nc + core
    _, rank = slot_ranks(ids, experts, near * nc + core_of)
    seat = (near * nc + core_of)[None, :] * cap + rank
    seat = jnp.where(rank < 0, -1, seat)
    seats = jnp.arange(2 * nc * cap, dtype=jnp.int32)
    send = (seat[:, None, :] == seats[None, :, None]).astype(BF).reshape(-1, count)

    table = table.reshape(2 * top, nz, nc, tok_sub)
    table = lax.dynamic_slice_in_dim(table, core, 1, 2).reshape(2 * top, -1)
    lane = jnp.arange(nx * nc, dtype=jnp.int32)
    experts = ((lane // nc) * nz + here) * nc + lane % nc
    own_count = table.shape[1]
    match, rank = slot_ranks(
        table[:top].astype(jnp.int32),
        experts,
        is_near(jnp.arange(own_count, dtype=jnp.int32) // tok_sub),
    )
    gain = jnp.sum(jnp.where(match, table[None, top:], 0.0), axis=1)

    def blocks_of(value, places):
        value = value.reshape(-1, nz, tok_sub)
        value = lax.dynamic_slice_in_dim(jnp.concatenate([value, value], 1), here, nz, 1)
        return jnp.concatenate([value[:, k] for k in places], 1)

    def back_for(places):
        slot = jnp.arange(cap, dtype=jnp.int32)
        taken = blocks_of(rank, places)[:, None, :] == slot[None, :, None]
        back = jnp.where(taken, blocks_of(gain, places)[:, None, :], 0.0)
        return back.astype(BF).reshape(len(experts) * cap, -1)

    backs = back_for(far_places), back_for(near_places)

    send_rows = jnp.dot(send, column, preferred_element_type=F32)
    send_rows = (send_rows * (1.0 / ROW_SCALE)).astype(BF)
    rows = lax.all_to_all(send_rows, X, split_axis=0, concat_axis=0, tiled=True)
    far, near = expert(rows, gate_all, up_all, down_all, nr, nc * cap)
    chunks = [None] * nz

    def spread_out(out, back, places):
        returned = lax.all_to_all(out, XC, split_axis=0, concat_axis=0, tiled=True)
        mixed = contract(back, returned, ((0,), (0,))).astype(BF)
        for i, place in enumerate(places):
            chunks[place] = mixed[i * tok_sub : (i + 1) * tok_sub]

    spread_out(far, backs[0], far_places)
    right, left = pair_up(chunks, nz // 2), pair_down(chunks, nz // 2 - 1)
    right, left, near = lax.optimization_barrier((right, left, near))
    spread_out(near, backs[1], near_places)
    expert_mix = ring_sums(chunks, right, left)
    return (hidden_sum + expert_mix).astype(BF)[None]


def solution(mesh):
    devices = mesh.devices
    split = Mesh(devices.reshape(4, 2, 2, devices.shape[1] // 8, 2), ("rep",) + EP)
    placed = (
        P(EP, "rep"),
        P(EP, "rep"),
        P(EP, "rep"),
        P(EP),
        P(EP, "rep", None),
        P(("rep",) + EP, None),
        P(),
        P(EP, "rep", None),
        P(EP, "rep", None),
        P(EP, None, "rep"),
        P(EP, "rep", None),
        P(EP, "rep", None),
    )
    return jax.shard_map(
        on_device, mesh=split, in_specs=placed, out_specs=P(EP, "rep", None), check_vma=False
    )
```

```python
import functools

import jax
import jax.numpy as jnp
from jax import lax
from jax.experimental import pallas as pl
from jax.experimental.pallas import tpu as pltpu
from jax.sharding import Mesh, PartitionSpec as P

HS = 128
HOPS = 4
CAP = 3
VMEM_GRANT = 56 * 2**20
WEIGHT_SCALE = 2.0**19
ROW_SCALE = 2.0**9
BF = jnp.bfloat16
F16 = jnp.float16
F32 = jnp.float32
X = ("xh", "xl")
EP = ("xh", "xl", "z", "core")
XC = ("xh", "xl", "core")
XZ = ("xh", "xl", "z")
ZC = ("z", "core")


def from_earlier(value, by):
    chips = lax.axis_size(XZ)
    return lax.ppermute(value, XZ, [(i, i + by) for i in range(chips - by)])


def shift(value, axis, by):
    devices = lax.axis_size(axis)
    return lax.ppermute(value, axis, [(i, (i + by) % devices) for i in range(devices)])


def contract(left, right, dims):
    return lax.dot_general(left, right, (dims, ((), ())), preferred_element_type=F32)


def attention(queries, keys, values, doc_start):
    tok_ep = queries.shape[0]
    group_size = queries.shape[1] // HS
    cores = lax.axis_size("core")
    chips = -(-HOPS // cores)
    own = lax.all_gather(jnp.concatenate([keys, values], 1), "core", axis=0, tiled=True)
    both = jnp.concatenate([from_earlier(own, by) for by in range(chips, 0, -1)] + [own], 0)
    key_all, value_all = both[:, :HS], both[:, HS:]
    first = (lax.axis_index(XZ) - chips) * cores * tok_ep
    key_pos = first + jnp.arange(both.shape[0], dtype=jnp.int32)
    query_pos = lax.axis_index(EP) * tok_ep + jnp.arange(tok_ep, dtype=jnp.int32)
    key_mask = (key_pos[None, :] <= query_pos[:, None]) & (key_pos[None, :] >= doc_start[:, None])
    query_heads = queries.reshape(tok_ep, group_size, HS)
    score_vals = jnp.einsum("igd,jd->gij", query_heads, key_all, preferred_element_type=F32) * (
        1.0 / HS**0.5
    )
    score_vals = jnp.where(key_mask[None], score_vals, -jnp.inf)
    row_peak = jnp.max(score_vals, axis=-1, keepdims=True)
    prob_vals = jnp.exp(score_vals - row_peak)
    row_total = jnp.sum(prob_vals, axis=-1, keepdims=True)
    weighted = jnp.einsum("gij,jd->igd", prob_vals.astype(BF), value_all, preferred_element_type=F32)
    return (
        (weighted / jnp.transpose(row_total, (1, 0, 2))).reshape(tok_ep, group_size * HS).astype(BF)
    )


def slot_ranks(ids, experts, class_of):
    match = ids[None] == experts[:, None, None]
    hit = jnp.any(match, axis=1)
    step = jnp.arange(ids.shape[1], dtype=jnp.int32)
    before = (step[:, None] < step[None, :]) & (class_of[:, None] == class_of[None, :])
    rank = jnp.dot(hit.astype(BF), before.astype(BF), preferred_element_type=F32).astype(jnp.int32)
    return match, jnp.where(hit, rank, -1)


def expert_kernel(chunk, group, rows_ref, gate_ref, up_ref, down_ref, *refs):
    far_ref, near_ref, gate_vm, up_vm, down_vm, hidden_ref, sems = refs
    units, parts = gate_ref.shape[0], down_ref.shape[0]
    cols = down_ref.shape[2]
    steps = units // chunk
    copies = []
    for step in range(steps):
        at = pl.ds(step * chunk, chunk)
        copies.append((gate_ref.at[at], gate_vm.at[at]))
        copies.append((up_ref.at[at], up_vm.at[at]))
    for part in range(parts):
        copies.append((down_ref.at[part], down_vm.at[part]))
    copies = [pltpu.make_async_copy(*pair, sems.at[i]) for i, pair in enumerate(copies)]
    ahead = 4
    for copy in copies[:ahead]:
        copy.start()

    def arrived(i):
        copies[i].wait()
        if i + ahead < len(copies):
            copies[i + ahead].start()

    rows = rows_ref[...]
    for step in range(steps):
        arrived(2 * step)
        arrived(2 * step + 1)
        at = slice(step * chunk, (step + 1) * chunk)
        gate = contract(rows, gate_vm[at], ((1,), (1,)))
        up = contract(rows, up_vm[at], ((1,), (1,)))
        hidden_ref[:, at] = (gate / (1.0 + jnp.exp(-gate)) * up).astype(BF)
    hidden = hidden_ref[...]
    for part in range(parts):
        arrived(2 * steps + part)
        total = jnp.dot(hidden, down_vm[part], preferred_element_type=F32).astype(BF)
        at = slice(part * cols, (part + 1) * cols)
        for k in range(far_ref.shape[0] // group):
            begin = 2 * k * group
            far_ref[k * group : (k + 1) * group, at] = total[begin : begin + group]
            near_ref[k * group : (k + 1) * group, at] = total[begin + group : begin + 2 * group]


def expert(rows, gate, up, down, parts, group):
    count, width = rows.shape
    down = down.reshape(parts, -1, down.shape[1])
    chunk = min(256, gate.shape[0])
    vmem, hbm = pl.BlockSpec(memory_space=pltpu.VMEM), pl.BlockSpec(memory_space=pltpu.HBM)
    return pl.pallas_call(
        functools.partial(expert_kernel, chunk, group),
        in_specs=[vmem, hbm, hbm, hbm],
        out_specs=[vmem, vmem],
        out_shape=[jax.ShapeDtypeStruct((count // 2, width), BF)] * 2,
        scratch_shapes=[
            pltpu.VMEM(gate.shape, BF),
            pltpu.VMEM(up.shape, BF),
            pltpu.VMEM(down.shape, BF),
            pltpu.VMEM((count, gate.shape[0]), BF),
            pltpu.SemaphoreType.DMA((2 * (gate.shape[0] // chunk) + parts,)),
        ],
        compiler_params=pltpu.CompilerParams(vmem_limit_bytes=VMEM_GRANT),
        cost_estimate=pl.CostEstimate(
            flops=2 * count * (gate.size + up.size + down.size),
            bytes_accessed=2 * (2 * rows.size + gate.size + up.size + down.size),
            transcendentals=count * gate.shape[0],
        ),
    )(rows, gate, up, down)


def add_low(left, right):
    return (left.astype(F32) + right.astype(F32)).astype(BF)


def pair_up(chunks, k):
    places = len(chunks)
    return jnp.concatenate([chunks[k % places], chunks[(k - 1) % places]], 0)


def pair_down(chunks, k):
    places = len(chunks)
    return jnp.concatenate([chunks[-k % places], chunks[(1 - k) % places]], 0)


def ring_sums(chunks, right, left):
    half = len(chunks) // 2
    rows = chunks[0].shape[0]
    for k in range(half - 2, 0, -2):
        right = add_low(shift(right, "z", 2), pair_up(chunks, k))
        left = shift(left, "z", -2)
        if k > 2:
            left = add_low(left, pair_down(chunks, k - 1))
    last = shift(add_low(left[:rows], chunks[-1]), "z", -1)
    pieces = [left[rows:], shift(right[:rows], "z", 2), shift(right[rows:], "z", 1), last]
    return sum((p.astype(F32) for p in pieces), chunks[0].astype(F32))


def on_device(
    queries,
    keys,
    values,
    doc_start,
    residual,
    out_weight,
    norm_gain,
    gate_weight,
    up_weight,
    down_weight,
    route_ids,
    route_weights,
):
    nx, nz, nc, nr = (lax.axis_size(a) for a in (X, "z", "core", "rep"))
    width = out_weight.shape[1]
    rows8 = out_weight.shape[0]
    tok_sub, top = route_ids.shape[1], route_ids.shape[2]
    here = lax.axis_index("z")

    gate_all = lax.all_gather(gate_weight[0], "rep", axis=0, tiled=True)
    up_all = lax.all_gather(up_weight[0], "rep", axis=0, tiled=True)
    down_all = lax.all_gather(down_weight[0], "rep", axis=0, tiled=True)

    own_rows = (out_weight * WEIGHT_SCALE).astype(F16)
    pair_rows = jnp.concatenate([own_rows, shift(own_rows, "xl", 1)], 0)
    info = jnp.concatenate([route_ids[0].astype(F16), route_weights[0].astype(F16)], 1)
    info = jnp.pad(info, ((0, 0), (0, 128 - 2 * top)))
    groups = tok_sub // (2 * rows8)
    info = [info[g * 2 * rows8 : (g + 1) * 2 * rows8] for g in range(groups)]
    pair_rows = jnp.concatenate([pair_rows] + info, 1)

    attended = attention(queries, keys, values, doc_start)
    half = attended.shape[1] // 2
    xh = lax.axis_index("xh")
    low, high = attended[:, :half], attended[:, half:]
    kept = jnp.where(xh == 0, low, high)
    given = jnp.where(xh == 0, high, low)
    got = shift(given, "xh", 1)
    pair_rows, _ = lax.optimization_barrier((pair_rows, given))
    z_all = lax.all_gather(pair_rows, ZC, axis=0, tiled=True)
    out_rows = z_all[:, :width].astype(BF)

    both = jnp.stack([jnp.where(xh == 0, kept, got), jnp.where(xh == 0, got, kept)], 0)
    both = both.reshape(2, nr, tok_sub, half).transpose(1, 0, 2, 3).reshape(-1, half)
    place = jnp.arange(half, dtype=jnp.int32)
    pi, px = place % rows8, place // rows8 % 2
    px = jnp.where(lax.axis_index("xl") == 0, px, 1 - px)
    pc, pz = place // (2 * rows8) % nc, place // (2 * rows8 * nc)
    source = ((px * nz + pz) * nc + pc) * rows8 + pi
    permute = (place[:, None] == source[None, :]).astype(BF)
    both = jnp.dot(both, permute, preferred_element_type=F32).astype(BF)
    partial_value = jnp.dot(both, out_rows, preferred_element_type=F32)
    partial_value = (partial_value * (1.0 / WEIGHT_SCALE)).astype(BF)
    parts = lax.all_to_all(partial_value, ("rep", "xh"), split_axis=0, concat_axis=0, tiled=True)
    head_total = jnp.sum(parts.reshape(-1, tok_sub, width).astype(F32), axis=0)
    hidden_sum = residual[0].astype(F32) + head_total
    inverse_rms = lax.rsqrt(jnp.mean(hidden_sum * hidden_sum, axis=-1, keepdims=True) + 1e-06)
    normed = (hidden_sum * inverse_rms * norm_gain).astype(BF)
    column = (normed * ROW_SCALE).astype(F16)
    column = lax.all_gather(column, ZC, axis=0, tiled=True).astype(BF)

    table = [z_all[:, width + 128 * g :][:, : 2 * top].astype(F32) for g in range(groups)]
    table = jnp.stack([jnp.transpose(t).reshape(2 * top, -1, 2 * rows8) for t in table], 2)
    table = table.reshape(2 * top, -1)
    count = table.shape[1]
    core = lax.axis_index("core")
    lanes = jnp.arange(count, dtype=jnp.int32)
    core_of = lanes // tok_sub % nc
    near_places = list(range(nz - nz // 4 + 1, nz)) + list(range(nz // 4 + 1))
    far_places = list(range(nz // 4 + 1, nz - nz // 4 + 1))
    cap = CAP * nz // 2

    def is_near(place):
        offset = (place - here + nz) % nz
        return ((offset <= nz // 4) | (offset > nz - nz // 4)).astype(jnp.int32)

    near = is_near(lanes // (tok_sub * nc))
    ids = table[:top].astype(jnp.int32)
    experts = (jnp.arange(nx, dtype=jnp.int32) * nz + here) * nc + core
    _, rank = slot_ranks(ids, experts, near * nc + core_of)
    seat = (near * nc + core_of)[None, :] * cap + rank
    seat = jnp.where(rank < 0, -1, seat)
    seats = jnp.arange(2 * nc * cap, dtype=jnp.int32)
    send = (seat[:, None, :] == seats[None, :, None]).astype(BF).reshape(-1, count)

    table = table.reshape(2 * top, nz, nc, tok_sub)
    table = lax.dynamic_slice_in_dim(table, core, 1, 2).reshape(2 * top, -1)
    lane = jnp.arange(nx * nc, dtype=jnp.int32)
    experts = ((lane // nc) * nz + here) * nc + lane % nc
    own_count = table.shape[1]
    match, rank = slot_ranks(
        table[:top].astype(jnp.int32),
        experts,
        is_near(jnp.arange(own_count, dtype=jnp.int32) // tok_sub),
    )
    gain = jnp.sum(jnp.where(match, table[None, top:], 0.0), axis=1)

    send_rows = jnp.dot(send, column, preferred_element_type=F32)
    send_rows = (send_rows * (1.0 / ROW_SCALE)).astype(BF)
    rows = lax.all_to_all(send_rows, X, split_axis=0, concat_axis=0, tiled=True)
    rows, rank, gain = lax.optimization_barrier((rows, rank, gain))

    def blocks_of(value, places):
        value = value.reshape(-1, nz, tok_sub)
        value = lax.dynamic_slice_in_dim(jnp.concatenate([value, value], 1), here, nz, 1)
        return jnp.concatenate([value[:, k] for k in places], 1)

    def back_for(places):
        slot = jnp.arange(cap, dtype=jnp.int32)
        taken = blocks_of(rank, places)[:, None, :] == slot[None, :, None]
        back = jnp.where(taken, blocks_of(gain, places)[:, None, :], 0.0)
        return back.astype(BF).reshape(len(experts) * cap, -1)

    backs = back_for(far_places), back_for(near_places)

    far, near = expert(rows, gate_all, up_all, down_all, nr, nc * cap)
    chunks = [None] * nz

    def spread_out(out, back, places):
        returned = lax.all_to_all(out, XC, split_axis=0, concat_axis=0, tiled=True)
        mixed = contract(back, returned, ((0,), (0,))).astype(BF)
        for i, place in enumerate(places):
            chunks[place] = mixed[i * tok_sub : (i + 1) * tok_sub]

    spread_out(far, backs[0], far_places)
    right, left = pair_up(chunks, nz // 2), pair_down(chunks, nz // 2 - 1)
    right, left, near = lax.optimization_barrier((right, left, near))
    spread_out(near, backs[1], near_places)
    expert_mix = ring_sums(chunks, right, left)
    return (hidden_sum + expert_mix).astype(BF)[None]


def solution(mesh):
    devices = mesh.devices
    split = Mesh(devices.reshape(4, 2, 2, devices.shape[1] // 8, 2), ("rep",) + EP)
    placed = (
        P(EP, "rep"),
        P(EP, "rep"),
        P(EP, "rep"),
        P(EP),
        P(EP, "rep", None),
        P(("rep",) + EP, None),
        P(),
        P(EP, "rep", None),
        P(EP, "rep", None),
        P(EP, None, "rep"),
        P(EP, "rep", None),
        P(EP, "rep", None),
    )
    return jax.shard_map(
        on_device, mesh=split, in_specs=placed, out_specs=P(EP, "rep", None), check_vma=False
    )
```

```python
import functools

import jax
import jax.numpy as jnp
from jax import lax
from jax.experimental import pallas as pl
from jax.experimental.pallas import tpu as pltpu
from jax.sharding import Mesh, PartitionSpec as P

HS = 128
HOPS = 4
CAP = 3
VMEM_GRANT = 56 * 2**20
WEIGHT_SCALE = 2.0**19
ROW_SCALE = 2.0**9
BF = jnp.bfloat16
F16 = jnp.float16
F32 = jnp.float32
X = ("xh", "xl")
EP = ("xh", "xl", "z", "core")
XC = ("xh", "xl", "core")
XZ = ("xh", "xl", "z")
ZC = ("z", "core")


def from_earlier(value, by):
    chips = lax.axis_size(XZ)
    return lax.ppermute(value, XZ, [(i, i + by) for i in range(chips - by)])


def shift(value, axis, by):
    devices = lax.axis_size(axis)
    return lax.ppermute(value, axis, [(i, (i + by) % devices) for i in range(devices)])


def contract(left, right, dims):
    return lax.dot_general(left, right, (dims, ((), ())), preferred_element_type=F32)


def attention(queries, keys, values, doc_start):
    tok_ep = queries.shape[0]
    group_size = queries.shape[1] // HS
    cores = lax.axis_size("core")
    chips = -(-HOPS // cores)
    own = lax.all_gather(jnp.concatenate([keys, values], 1), "core", axis=0, tiled=True)
    both = jnp.concatenate([from_earlier(own, by) for by in range(chips, 0, -1)] + [own], 0)
    key_all, value_all = both[:, :HS], both[:, HS:]
    first = (lax.axis_index(XZ) - chips) * cores * tok_ep
    key_pos = first + jnp.arange(both.shape[0], dtype=jnp.int32)
    query_pos = lax.axis_index(EP) * tok_ep + jnp.arange(tok_ep, dtype=jnp.int32)
    key_mask = (key_pos[None, :] <= query_pos[:, None]) & (key_pos[None, :] >= doc_start[:, None])
    query_heads = queries.reshape(tok_ep, group_size, HS)
    score_vals = jnp.einsum("igd,jd->gij", query_heads, key_all, preferred_element_type=F32) * (
        1.0 / HS**0.5
    )
    score_vals = jnp.where(key_mask[None], score_vals, -jnp.inf)
    row_peak = jnp.max(score_vals, axis=-1, keepdims=True)
    prob_vals = jnp.exp(score_vals - row_peak)
    row_total = jnp.sum(prob_vals, axis=-1, keepdims=True)
    weighted = jnp.einsum("gij,jd->igd", prob_vals.astype(BF), value_all, preferred_element_type=F32)
    return (
        (weighted / jnp.transpose(row_total, (1, 0, 2))).reshape(tok_ep, group_size * HS).astype(BF)
    )


def slot_ranks(ids, experts, class_of):
    match = ids[None] == experts[:, None, None]
    hit = jnp.any(match, axis=1)
    step = jnp.arange(ids.shape[1], dtype=jnp.int32)
    before = (step[:, None] < step[None, :]) & (class_of[:, None] == class_of[None, :])
    rank = jnp.dot(hit.astype(BF), before.astype(BF), preferred_element_type=F32).astype(jnp.int32)
    return match, jnp.where(hit, rank, -1)


def expert_kernel(chunk, group, rows_ref, gate_ref, up_ref, down_ref, *refs):
    far_ref, near_ref, gate_vm, up_vm, down_vm, hidden_ref, sems = refs
    units, parts = gate_ref.shape[0], down_ref.shape[0]
    cols = down_ref.shape[2]
    steps = units // chunk
    copies = []
    for step in range(steps):
        at = pl.ds(step * chunk, chunk)
        copies.append((gate_ref.at[at], gate_vm.at[at]))
        copies.append((up_ref.at[at], up_vm.at[at]))
    for part in range(parts):
        copies.append((down_ref.at[part], down_vm.at[part]))
    copies = [pltpu.make_async_copy(*pair, sems.at[i]) for i, pair in enumerate(copies)]
    ahead = 4
    for copy in copies[:ahead]:
        copy.start()

    def arrived(i):
        copies[i].wait()
        if i + ahead < len(copies):
            copies[i + ahead].start()

    rows = rows_ref[...]
    for step in range(steps):
        arrived(2 * step)
        arrived(2 * step + 1)
        at = slice(step * chunk, (step + 1) * chunk)
        gate = contract(rows, gate_vm[at], ((1,), (1,)))
        up = contract(rows, up_vm[at], ((1,), (1,)))
        hidden_ref[:, at] = (gate / (1.0 + jnp.exp(-gate)) * up).astype(BF)
    hidden = hidden_ref[...]
    for part in range(parts):
        arrived(2 * steps + part)
        total = jnp.dot(hidden, down_vm[part], preferred_element_type=F32).astype(BF)
        at = slice(part * cols, (part + 1) * cols)
        for k in range(far_ref.shape[0] // group):
            begin = 2 * k * group
            far_ref[k * group : (k + 1) * group, at] = total[begin : begin + group]
            near_ref[k * group : (k + 1) * group, at] = total[begin + group : begin + 2 * group]


def expert(rows, gate, up, down, parts, group):
    count, width = rows.shape
    down = down.reshape(parts, -1, down.shape[1])
    chunk = min(256, gate.shape[0])
    vmem, hbm = pl.BlockSpec(memory_space=pltpu.VMEM), pl.BlockSpec(memory_space=pltpu.HBM)
    return pl.pallas_call(
        functools.partial(expert_kernel, chunk, group),
        in_specs=[vmem, hbm, hbm, hbm],
        out_specs=[vmem, vmem],
        out_shape=[jax.ShapeDtypeStruct((count // 2, width), BF)] * 2,
        scratch_shapes=[
            pltpu.VMEM(gate.shape, BF),
            pltpu.VMEM(up.shape, BF),
            pltpu.VMEM(down.shape, BF),
            pltpu.VMEM((count, gate.shape[0]), BF),
            pltpu.SemaphoreType.DMA((2 * (gate.shape[0] // chunk) + parts,)),
        ],
        compiler_params=pltpu.CompilerParams(vmem_limit_bytes=VMEM_GRANT),
        cost_estimate=pl.CostEstimate(
            flops=2 * count * (gate.size + up.size + down.size),
            bytes_accessed=2 * (2 * rows.size + gate.size + up.size + down.size),
            transcendentals=count * gate.shape[0],
        ),
    )(rows, gate, up, down)


def add_low(left, right):
    return (left.astype(F32) + right.astype(F32)).astype(BF)


def pair_up(chunks, k):
    places = len(chunks)
    return jnp.concatenate([chunks[k % places], chunks[(k - 1) % places]], 0)


def pair_down(chunks, k):
    places = len(chunks)
    return jnp.concatenate([chunks[-k % places], chunks[(1 - k) % places]], 0)


def ring_sums(chunks, right, left):
    half = len(chunks) // 2
    rows = chunks[0].shape[0]
    for k in range(half - 2, 0, -2):
        right = add_low(shift(right, "z", 2), pair_up(chunks, k))
        left = shift(left, "z", -2)
        if k > 2:
            left = add_low(left, pair_down(chunks, k - 1))
    last = shift(add_low(left[:rows], chunks[-1]), "z", -1)
    pieces = [left[rows:], shift(right[:rows], "z", 2), shift(right[rows:], "z", 1), last]
    return sum((p.astype(F32) for p in pieces), chunks[0].astype(F32))


def on_device(
    queries,
    keys,
    values,
    doc_start,
    residual,
    out_weight,
    norm_gain,
    gate_weight,
    up_weight,
    down_weight,
    route_ids,
    route_weights,
):
    nx, nz, nc, nr = (lax.axis_size(a) for a in (X, "z", "core", "rep"))
    width = out_weight.shape[1]
    rows8 = out_weight.shape[0]
    tok_sub, top = route_ids.shape[1], route_ids.shape[2]
    here = lax.axis_index("z")

    gate_all = lax.all_gather(gate_weight[0], "rep", axis=0, tiled=True)
    up_all = lax.all_gather(up_weight[0], "rep", axis=0, tiled=True)
    down_all = lax.all_gather(down_weight[0], "rep", axis=0, tiled=True)

    own_rows = (out_weight * WEIGHT_SCALE).astype(F16)
    pair_rows = jnp.concatenate([own_rows, shift(own_rows, "xl", 1)], 0)
    info = jnp.concatenate([route_ids[0].astype(F16), route_weights[0].astype(F16)], 1)
    info = jnp.pad(info, ((0, 0), (0, 128 - 2 * top)))
    groups = tok_sub // (2 * rows8)
    info = [info[g * 2 * rows8 : (g + 1) * 2 * rows8] for g in range(groups)]
    pair_rows = jnp.concatenate([pair_rows] + info, 1)

    attended = attention(queries, keys, values, doc_start)
    half = attended.shape[1] // 2
    xh = lax.axis_index("xh")
    low, high = attended[:, :half], attended[:, half:]
    kept = jnp.where(xh == 0, low, high)
    given = jnp.where(xh == 0, high, low)
    got = shift(given, "xh", 1)
    pair_rows, _ = lax.optimization_barrier((pair_rows, given))
    z_all = lax.all_gather(pair_rows, ZC, axis=0, tiled=True)
    out_rows = z_all[:, :width].astype(BF)

    both = jnp.stack([jnp.where(xh == 0, kept, got), jnp.where(xh == 0, got, kept)], 0)
    both = both.reshape(2, nr, tok_sub, half).transpose(1, 0, 2, 3).reshape(-1, half)
    place = jnp.arange(half, dtype=jnp.int32)
    pi, px = place % rows8, place // rows8 % 2
    px = jnp.where(lax.axis_index("xl") == 0, px, 1 - px)
    pc, pz = place // (2 * rows8) % nc, place // (2 * rows8 * nc)
    source = ((px * nz + pz) * nc + pc) * rows8 + pi
    permute = (place[:, None] == source[None, :]).astype(BF)
    both = jnp.dot(both, permute, preferred_element_type=F32).astype(BF)
    partial_value = jnp.dot(both, out_rows, preferred_element_type=F32)
    partial_value = (partial_value * (1.0 / WEIGHT_SCALE)).astype(BF)
    parts = lax.all_to_all(partial_value, ("rep", "xh"), split_axis=0, concat_axis=0, tiled=True)
    head_total = jnp.sum(parts.reshape(-1, tok_sub, width).astype(F32), axis=0)
    hidden_sum = residual[0].astype(F32) + head_total
    inverse_rms = lax.rsqrt(jnp.mean(hidden_sum * hidden_sum, axis=-1, keepdims=True) + 1e-06)
    normed = (hidden_sum * inverse_rms * norm_gain).astype(BF)
    column = (normed * ROW_SCALE).astype(F16)
    column = lax.all_gather(column, ZC, axis=0, tiled=True).astype(BF)

    table = [z_all[:, width + 128 * g :][:, : 2 * top].astype(F32) for g in range(groups)]
    table = jnp.stack([jnp.transpose(t).reshape(2 * top, -1, 2 * rows8) for t in table], 2)
    table = table.reshape(2 * top, -1)
    count = table.shape[1]
    core = lax.axis_index("core")
    lanes = jnp.arange(count, dtype=jnp.int32)
    core_of = lanes // tok_sub % nc
    near_places = list(range(nz - nz // 4 + 1, nz)) + list(range(nz // 4 + 1))
    far_places = list(range(nz // 4 + 1, nz - nz // 4 + 1))
    cap = CAP * nz // 2

    def is_near(place):
        offset = (place - here + nz) % nz
        return ((offset <= nz // 4) | (offset > nz - nz // 4)).astype(jnp.int32)

    near = is_near(lanes // (tok_sub * nc))
    ids = table[:top].astype(jnp.int32)
    experts = (jnp.arange(nx, dtype=jnp.int32) * nz + here) * nc + core
    _, rank = slot_ranks(ids, experts, near * nc + core_of)
    seat = (near * nc + core_of)[None, :] * cap + rank
    seat = jnp.where(rank < 0, -1, seat)
    seats = jnp.arange(2 * nc * cap, dtype=jnp.int32)
    send = (seat[:, None, :] == seats[None, :, None]).astype(BF).reshape(-1, count)

    send_rows = jnp.dot(send, column, preferred_element_type=F32)
    send_rows = (send_rows * (1.0 / ROW_SCALE)).astype(BF)
    rows = lax.all_to_all(send_rows, X, split_axis=0, concat_axis=0, tiled=True)
    rows, table = lax.optimization_barrier((rows, table))

    table = table.reshape(2 * top, nz, nc, tok_sub)
    table = lax.dynamic_slice_in_dim(table, core, 1, 2).reshape(2 * top, -1)
    lane = jnp.arange(nx * nc, dtype=jnp.int32)
    experts = ((lane // nc) * nz + here) * nc + lane % nc
    own_count = table.shape[1]
    match, rank = slot_ranks(
        table[:top].astype(jnp.int32),
        experts,
        is_near(jnp.arange(own_count, dtype=jnp.int32) // tok_sub),
    )
    gain = jnp.sum(jnp.where(match, table[None, top:], 0.0), axis=1)

    def blocks_of(value, places):
        value = value.reshape(-1, nz, tok_sub)
        value = lax.dynamic_slice_in_dim(jnp.concatenate([value, value], 1), here, nz, 1)
        return jnp.concatenate([value[:, k] for k in places], 1)

    def back_for(places):
        slot = jnp.arange(cap, dtype=jnp.int32)
        taken = blocks_of(rank, places)[:, None, :] == slot[None, :, None]
        back = jnp.where(taken, blocks_of(gain, places)[:, None, :], 0.0)
        return back.astype(BF).reshape(len(experts) * cap, -1)

    backs = back_for(far_places), back_for(near_places)

    far, near = expert(rows, gate_all, up_all, down_all, nr, nc * cap)
    chunks = [None] * nz

    def spread_out(out, back, places):
        returned = lax.all_to_all(out, XC, split_axis=0, concat_axis=0, tiled=True)
        mixed = contract(back, returned, ((0,), (0,))).astype(BF)
        for i, place in enumerate(places):
            chunks[place] = mixed[i * tok_sub : (i + 1) * tok_sub]

    spread_out(far, backs[0], far_places)
    right, left = pair_up(chunks, nz // 2), pair_down(chunks, nz // 2 - 1)
    right, left, near = lax.optimization_barrier((right, left, near))
    spread_out(near, backs[1], near_places)
    expert_mix = ring_sums(chunks, right, left)
    return (hidden_sum + expert_mix).astype(BF)[None]


def solution(mesh):
    devices = mesh.devices
    split = Mesh(devices.reshape(4, 2, 2, devices.shape[1] // 8, 2), ("rep",) + EP)
    placed = (
        P(EP, "rep"),
        P(EP, "rep"),
        P(EP, "rep"),
        P(EP),
        P(EP, "rep", None),
        P(("rep",) + EP, None),
        P(),
        P(EP, "rep", None),
        P(EP, "rep", None),
        P(EP, None, "rep"),
        P(EP, "rep", None),
        P(EP, "rep", None),
    )
    return jax.shard_map(
        on_device, mesh=split, in_specs=placed, out_specs=P(EP, "rep", None), check_vma=False
    )
```
